512 devices in a mesh: tile: 64 (over z, y_lo, core), seq: 8 (over x, y_hi).
Axes of the slice: x: 4, y: 4 (y_hi: 2, y_lo: 2; y = y_hi * 2 + y_lo), z: 16, core: 2. Of those that a mesh axis runs over, the one named last changes fastest.
Arguments:
- tokens: bfloat16 [64, 2048, 1152], P('tile', 'seq'), may hold values from -6 to 6
- mod_shift: float32 [64, 1152], P('tile'), may hold values from -3 to 3
- mod_scale: float32 [64, 1152], P('tile'), may hold values from -0.9 to 3.5
- mod_gate: float32 [64, 1152], P('tile'), may hold values from -6 to 6
- w_qkv: bfloat16 [3, 1152, 576], P(None, None, 'seq'), may hold values from -0.29882812 to 0.29882812
- w_out: bfloat16 [576, 1152], P('seq'), may hold values from -0.25 to 0.25
- east_rows: int32 [64, 256], P('tile', 'seq'), may hold values from 0 to 255, as said below
- west_rows: int32 [64, 256], P('tile', 'seq'), may hold values from 0 to 255, as said below
- blend_weight: int32 [64, 256], P(None, 'seq'), may hold values from 1 to 7
Outputs:
- blended: bfloat16 [64, 2048, 1152], P('tile', 'seq')
The draws below stay inside these ranges and needn't reach their ends.
Inputs may be any that keep to these rules, and one draw needn't show every extreme that they name: In each tile and each block of 32 entries (one block of 256 tokens), the east_rows entries are distinct and none equals a west_rows entry of the same block. `west_rows`: distinct within each block of 32 entries, disjoint from east_rows of the same block.
All inputs are finite; a program needn't handle non-finite values.
Results may differ from the reference program's by a relative error of at most 0.02.
Values may be sent and summed in bfloat16 or wider, within the bound.
No kernel may reach another device: no remote copies, remote signals or barrier semaphores. Data moves between devices by JAX's collectives and lax.ppermute only.
A program may use at most 64 MiB of HBM per device.

```python
import jax
import jax.numpy as jnp
from jax import lax

D = 1152
HD = 72
HEADS = 8
HQ = 576
TOK_DEV = 256
OV = 32
TILE_TOK = 2048
TILES = 64
N_SEQ = 8


def margin_order(key):
    group = TILE_TOK // TOK_DEV
    keys = jax.random.split(key, TILES * group)
    orders = jax.vmap(lambda single: jax.random.permutation(single, TOK_DEV))(keys)
    return orders.reshape(TILES, group, TOK_DEV).astype(jnp.int32)


def draw_east_rows(key, part):
    orders = margin_order(key)
    return orders[:, :, :OV].reshape(TILES, -1)


def draw_west_rows(key, part):
    orders = margin_order(key)
    return orders[:, :, OV:2 * OV].reshape(TILES, -1)


def draw_mod_scale(key, part):
    key = jax.random.fold_in(key, 7)
    return jnp.clip(0.4 * jax.random.normal(key, (TILES, D), jnp.float32), -0.9, 1.5)


def with_ends(values, key, low, high):
    longest = values.shape.index(max(values.shape))
    spots = []
    for shift in (0, 1):
        where = [jax.random.randint(jax.random.fold_in(key, axis), (), 0, length) for axis, length in enumerate(values.shape)]
        where[longest] = (where[longest] + shift) % values.shape[longest]
        spots.append(tuple(where))
    return values.at[spots[0]].set(low).at[spots[1]].set(high)


def block_scale(stream_key, extent, shards, smallest, top_value):
    def one(position, shards_of):
        heights = jax.random.uniform(jax.random.fold_in(jax.random.fold_in(stream_key, 6), position), (shards_of,), jnp.float32, smallest / len(shards), top_value / len(shards))
        return jnp.repeat(jnp.exp(heights), extent[position] // shards_of).reshape((-1,) + (1,) * (len(extent) - position - 1))

    factor_of = one(*shards[0])
    for cut in shards[1:]:
        factor_of = factor_of * one(*cut)
    return factor_of


def scatter_about(key, dims, spread, most, pieces=(), held_as=jnp.bfloat16):
    gain = block_scale(key, dims, pieces, -0.22, 0.18) if pieces else 1.0
    drawn = jax.random.normal(key, dims, jnp.float32) * spread * gain
    return jnp.minimum(jnp.maximum(drawn, -most), most).astype(held_as)


def setup_inputs(seed: int = 0) -> dict:
    key_of = jax.random.split(jax.random.key(seed), 10)
    tokens = scatter_about(key_of[0], (TILES, TILE_TOK, D), 1.0, 6.0, ((0, 64), (1, 8)))
    mod_shift = scatter_about(key_of[1], (TILES, D), 0.5, 3.0, ((0, 64),), jnp.float32)
    mod_scale = draw_mod_scale(jax.random.fold_in(key_of[9], 71), 0)
    mod_gate = scatter_about(key_of[3], (TILES, D), 1.5, 6.0, ((0, 64),), jnp.float32)
    w_qkv = scatter_about(key_of[4], (3, D, HQ), 0.05, 0.29882812, ((2, 8),))
    w_out = scatter_about(key_of[5], (HQ, D), HQ ** -0.5, 0.25, ((0, 8),))
    east_rows = draw_east_rows(jax.random.fold_in(key_of[9], 71), 0)
    west_rows = draw_west_rows(jax.random.fold_in(key_of[9], 71), 0)
    blend_weight = with_ends(jax.random.randint(key_of[8], (TILES, N_SEQ * OV), 1, 8), jax.random.fold_in(key_of[8], 1), 1, 7).astype(jnp.int32)
    return dict(tokens=tokens, mod_shift=mod_shift, mod_scale=mod_scale, mod_gate=mod_gate, w_qkv=w_qkv, w_out=w_out, east_rows=east_rows, west_rows=west_rows, blend_weight=blend_weight)


def layer_norm(values):
    mean = lax.optimization_barrier(jnp.mean(values, axis=-1, keepdims=True))
    centered = values - mean
    var = lax.optimization_barrier(jnp.mean(centered * centered, axis=-1, keepdims=True))
    return centered * lax.rsqrt(var + 1e-06)

def reference(tokens, mod_shift, mod_scale, mod_gate, w_qkv, w_out, east_rows, west_rows, blend_weight):

    def tile_layer(inputs):
        x_tile, shift, scale, gate = inputs
        normed = layer_norm(x_tile.astype(jnp.float32))
        modulated = (normed * (1.0 + scale) + shift).astype(jnp.bfloat16)
        query = jnp.dot(modulated, w_qkv[0], preferred_element_type=jnp.float32).astype(jnp.bfloat16)
        keys = jnp.dot(modulated, w_qkv[1], preferred_element_type=jnp.float32).astype(jnp.bfloat16)
        values = jnp.dot(modulated, w_qkv[2], preferred_element_type=jnp.float32).astype(jnp.bfloat16)
        query = query.reshape(TILE_TOK, HEADS, HD).astype(jnp.float32)
        keys = keys.reshape(TILE_TOK, HEADS, HD).astype(jnp.float32)
        values = values.reshape(TILE_TOK, HEADS, HD).astype(jnp.float32)
        scores = jnp.einsum('qhd,khd->hqk', query, keys) * HD ** (-0.5)
        peak = lax.optimization_barrier(jnp.max(scores, axis=-1, keepdims=True))
        expo = jnp.exp(scores - peak)
        denom = lax.optimization_barrier(jnp.sum(expo, axis=-1))
        probs = expo.astype(jnp.bfloat16).astype(jnp.float32)
        summed = jnp.einsum('hqk,khd->qhd', probs, values)
        attn = (summed / jnp.transpose(denom)[:, :, None]).reshape(TILE_TOK, HQ).astype(jnp.bfloat16)
        proj = jnp.dot(attn, w_out, preferred_element_type=jnp.float32)
        return (x_tile.astype(jnp.float32) + gate * proj).astype(jnp.bfloat16)
    layer_out = lax.map(tile_layer, (tokens, mod_shift, mod_scale, mod_gate))
    base = (jnp.arange(N_SEQ, dtype=jnp.int32) * TOK_DEV)[:, None]
    east_index = (east_rows.reshape(TILES, N_SEQ, OV) + base).reshape(TILES, N_SEQ * OV).astype(jnp.int32)
    west_index = (west_rows.reshape(TILES, N_SEQ, OV) + base).reshape(TILES, N_SEQ * OV).astype(jnp.int32)
    own_east = jnp.take_along_axis(layer_out, east_index[:, :, None], axis=1).astype(jnp.float32)
    own_west = jnp.take_along_axis(layer_out, west_index[:, :, None], axis=1).astype(jnp.float32)
    next_west = jnp.roll(own_west, -1, axis=0)
    prev_east = jnp.roll(own_east, 1, axis=0)
    weight_east = blend_weight.astype(jnp.float32)[:, :, None]
    weight_west = jnp.roll(weight_east, 1, axis=0)
    new_east = (weight_east * own_east + (8.0 - weight_east) * next_west) / 8.0
    new_west = ((8.0 - weight_west) * own_west + weight_west * prev_east) / 8.0
    tile_index = jnp.arange(TILES, dtype=jnp.int32)[:, None]
    blended = layer_out.at[tile_index, east_index].set(new_east.astype(jnp.bfloat16))
    blended = blended.at[tile_index, west_index].set(new_west.astype(jnp.bfloat16))
    return blended
```

```python
import functools
import math

import jax
import jax.numpy as jnp
from jax import lax
from jax.experimental import pallas as pl
from jax.experimental.pallas import tpu as pltpu
from jax.sharding import Mesh
from jax.sharding import PartitionSpec as P

D = 1152
HD = 72
TOK = 256
OV = 32
TILE = ("z", "ylo", "core")
SEQ = ("x", "yhi")
VMEM = pl.BlockSpec(memory_space=pltpu.VMEM)
BF = jnp.bfloat16
F32 = jnp.float32


def call(kernel, outs, args, flops, nbytes, transcendentals=0, vmem=48):
    return pl.pallas_call(
        kernel,
        out_shape=outs,
        in_specs=[VMEM] * len(args),
        out_specs=jax.tree.map(lambda _: VMEM, outs),
        compiler_params=pltpu.CompilerParams(vmem_limit_bytes=vmem * 1024 * 1024),
        cost_estimate=pl.CostEstimate(
            flops=flops, bytes_accessed=nbytes, transcendentals=transcendentals
        ),
    )(*args)


def pack_kernel(w_ref, wo_ref, out_ref):
    core = lax.axis_index("core")

    def put(first, second):
        both = jnp.concatenate([first.astype(F32), second.astype(F32)], axis=0).astype(BF)
        for i in range(4):
            out_ref[i] = both

    @pl.when(core == 0)
    def _():
        put(w_ref[0], w_ref[1])

    @pl.when(core == 1)
    def _():
        put(w_ref[2], wo_ref[...])


def modulate(x_ref, shift, scale):
    x = x_ref[...].astype(F32)
    mean = jnp.sum(x, axis=-1, keepdims=True) * (1.0 / D)
    centered = x - mean
    var = jnp.sum(centered * centered, axis=-1, keepdims=True) * (1.0 / D)
    normed = centered * lax.rsqrt(var + 1e-06)
    return (normed * (1.0 + scale) + shift).astype(BF)


def norm_kernel(x_ref, xo_ref, shift_ref, scale_ref, out_ref):
    shift = shift_ref[...]
    scale = scale_ref[...]
    out_ref[:TOK] = modulate(x_ref, shift, scale)
    out_ref[TOK:] = modulate(xo_ref, shift, scale)


def qkv_kernel(mod_ref, mine_ref, other_ref, out_ref, wo_ref):
    core = lax.axis_index("core")
    mod = mod_ref[...]

    def go(qk_ref, vo_ref):
        for h in range(4):
            qk = lax.dot_general(
                qk_ref[h], mod, (((1,), (1,)), ((), ())), preferred_element_type=F32
            )
            vw = vo_ref[h]
            v = lax.dot_general(
                vw[:80], mod, (((1,), (1,)), ((), ())), preferred_element_type=F32
            )
            out_ref[h] = jnp.concatenate([qk, v[:HD]], axis=0).astype(BF)
            wo_ref[h] = vw.astype(F32)[HD:].astype(BF)

    @pl.when(core == 0)
    def _():
        go(mine_ref, other_ref)

    @pl.when(core == 1)
    def _():
        go(other_ref, mine_ref)


def attention_kernel(qkv_ref, out_ref):
    yhi = lax.axis_index("yhi")
    factor = math.log2(math.e) * HD**-0.5
    keys = []
    values = []
    queries = []
    ones = jnp.ones((8, 2 * TOK), F32)
    for b in range(4):
        block = qkv_ref[b].astype(F32)
        q = block[:HD] * factor
        hi = q.astype(BF).astype(F32)
        lo = q - hi
        k = block[HD : 2 * HD]
        queries.append(jnp.concatenate([hi, lo], axis=0).astype(BF))
        keys.append(jnp.concatenate([k, k], axis=0).T.astype(BF))
        values.append(jnp.concatenate([block[2 * HD :], ones], axis=0).astype(BF))
    k_all = jnp.concatenate(keys, axis=0)
    v_all = jnp.concatenate(values, axis=1)
    for b in range(4):
        for half in range(2):
            q = queries[b][:, half * TOK : (half + 1) * TOK]
            s = jnp.dot(k_all, q, preferred_element_type=F32)
            peak = jnp.max(s, axis=0, keepdims=True)
            p = jnp.exp2(s - peak).astype(BF)
            o = jnp.dot(v_all, p, preferred_element_type=F32)
            res = (o[:HD] / o[HD : HD + 1]).astype(BF)
            owner = yhi if half == 0 else 1 - yhi
            out_ref[owner * 4 + b] = res


def column(row):
    size = row.shape[1]
    eye = lax.broadcasted_iota(jnp.int32, (size, size), 0) == lax.broadcasted_iota(
        jnp.int32, (size, size), 1
    )
    return jnp.sum(jnp.where(eye, row.astype(F32), 0.0), axis=1, keepdims=True)


def select_rows(east_ref, west_ref):
    e = column(east_ref[...])
    w = column(west_ref[...])
    rows = jnp.concatenate([e, w], axis=0).astype(jnp.int32)
    return jnp.where(
        lax.broadcasted_iota(jnp.int32, (2 * OV, TOK), 1) == rows, 1.0, 0.0
    ).astype(BF)


def project(attn, wo):
    return lax.dot_general(attn, wo, (((0,), (0,)), ((), ())), preferred_element_type=F32)


def margin_kernel(attn_ref, wo_ref, wo2_ref, x_ref, gate_ref, east_ref, west_ref, e_ref, w_ref):
    yhi = lax.axis_index("yhi")
    pick = select_rows(east_ref, west_ref)
    nt = (((1,), (1,)), ((), ()))
    mine = lax.dot_general(pick, attn_ref[yhi], nt, preferred_element_type=F32).astype(BF)
    other = lax.dot_general(pick, attn_ref[1 - yhi], nt, preferred_element_type=F32).astype(BF)
    x = jnp.dot(pick, x_ref[...], preferred_element_type=F32)
    proj = jnp.dot(mine, wo_ref[...], preferred_element_type=F32) + jnp.dot(
        other, wo2_ref[...], preferred_element_type=F32
    )
    rows = (x + gate_ref[...] * proj).astype(BF)
    e_ref[...] = rows[:OV]
    w_ref[...] = rows[OV:]


def out_kernel(attn_ref, wo_ref, wo2_ref, x_ref, gate_ref, out_ref):
    yhi = lax.axis_index("yhi")
    proj = project(attn_ref[yhi], wo_ref[...]) + project(attn_ref[1 - yhi], wo2_ref[...])
    out_ref[...] = (x_ref[...].astype(F32) + gate_ref[...] * proj).astype(BF)


def blend_kernel(lay_ref, e_ref, w_ref, prev_ref, next_ref, east_ref, west_ref, bw_ref, out_ref):
    tile = lax.axis_index("z") * 4 + lax.axis_index("ylo") * 2 + lax.axis_index("core")
    prior = jnp.where(tile == 0, 63, tile - 1)
    a_e = column(bw_ref[pl.ds(tile, 1), :])
    a_w = column(bw_ref[pl.ds(prior, 1), :])
    new_e = (a_e * e_ref[...].astype(F32) + (8.0 - a_e) * next_ref[...].astype(F32)) / 8.0
    new_w = ((8.0 - a_w) * w_ref[...].astype(F32) + a_w * prev_ref[...].astype(F32)) / 8.0
    new = jnp.concatenate([new_e, new_w], axis=0).astype(BF)
    index = jnp.concatenate([east_ref[...], west_ref[...]], axis=1)
    hot = jnp.where(
        lax.broadcasted_iota(jnp.int32, (TOK, 2 * OV), 0) == index, 1.0, 0.0
    )
    mask = jnp.sum(hot, axis=1, keepdims=True)
    placed = jnp.dot(hot.astype(BF), new, preferred_element_type=F32)
    out_ref[...] = jnp.where(mask > 0.5, placed, lay_ref[...].astype(F32)).astype(BF)


def body(tokens, mod_shift, mod_scale, mod_gate, w_qkv, w_out, east_rows, west_rows, blend_weight):
    sds = jax.ShapeDtypeStruct
    x = tokens[0]
    swap = [(0, 1), (1, 0)]
    x_other = lax.ppermute(x, "yhi", swap)
    packed = call(
        pack_kernel,
        sds((4, 2 * HD, D), BF),
        (jnp.transpose(w_qkv, (0, 2, 1)), w_out),
        1000,
        2000000,
    )
    mine = lax.all_to_all(packed, "x", 0, 0, tiled=True)
    mine, x_other = lax.optimization_barrier((mine, x_other))
    other = lax.ppermute(mine, "core", swap)
    mod = call(
        norm_kernel,
        sds((2 * TOK, D), BF),
        (x, x_other, mod_shift, mod_scale),
        20 * 512 * D,
        3000000,
    )
    qkv, wo = call(
        qkv_kernel,
        (sds((4, 3 * HD, 2 * TOK), BF), sds((4, HD, D), BF)),
        (mod, mine, other),
        2 * 512 * 896 * D,
        6000000,
    )
    pairs = [(0, 3), (3, 0), (1, 2), (2, 1)]
    wo_other = lax.ppermute(wo, ("ylo", "yhi"), pairs)
    qkv = lax.all_to_all(qkv, "x", 0, 0, tiled=True)
    attn = call(
        attention_kernel,
        sds((8, HD, TOK), BF),
        (qkv,),
        4 * 2048 * 2048 * 128,
        1500000,
        2048 * 2048,
    )
    attn = lax.all_to_all(attn, ("yhi", "x"), 0, 0, tiled=True).reshape(2, 4 * HD, TOK)
    wo = wo.reshape(4 * HD, D)
    wo_other = wo_other.reshape(4 * HD, D)
    own_e, own_w = call(
        margin_kernel,
        (sds((OV, D), BF), sds((OV, D), BF)),
        (attn, wo, wo_other, x, mod_gate, east_rows, west_rows),
        2 * 64 * 576 * D,
        2000000,
    )
    count = 64
    prev_e = lax.ppermute(own_e, TILE, [(i, (i + 1) % count) for i in range(count)])
    next_w = lax.ppermute(own_w, TILE, [(i, (i - 1) % count) for i in range(count)])
    lay = call(
        out_kernel,
        sds((TOK, D), BF),
        (attn, wo, wo_other, x, mod_gate),
        2 * 256 * 576 * D,
        3000000,
    )
    out = call(
        blend_kernel,
        sds((TOK, D), BF),
        (lay, own_e, own_w, prev_e, next_w, east_rows, west_rows, blend_weight),
        2 * 256 * 64 * D,
        1500000,
    )
    return out[None]


def solution(mesh):
    fine = Mesh(mesh.devices.reshape(16, 2, 2, 4, 2), ("z", "ylo", "core", "x", "yhi"))
    in_specs = (
        P(TILE, SEQ, None),
        P(TILE, None),
        P(TILE, None),
        P(TILE, None),
        P(None, None, SEQ),
        P(SEQ, None),
        P(TILE, SEQ),
        P(TILE, SEQ),
        P(None, SEQ),
    )
    out_specs = P(TILE, SEQ, None)
    return jax.shard_map(body, mesh=fine, in_specs=in_specs, out_specs=out_specs, check_vma=False)
```

```python
import functools
import math

import jax
import jax.numpy as jnp
from jax import lax
from jax.experimental import pallas as pl
from jax.experimental.pallas import tpu as pltpu
from jax.sharding import Mesh
from jax.sharding import PartitionSpec as P

D = 1152
HD = 72
TOK = 256
OV = 32
TILE = ("z", "ylo", "core")
SEQ = ("x", "yhi")
VMEM = pl.BlockSpec(memory_space=pltpu.VMEM)
HBM = pl.BlockSpec(memory_space=pltpu.HBM)
BF = jnp.bfloat16
F32 = jnp.float32


def call(kernel, outs, args, flops, nbytes, trans=0, ins=None, out_specs=None, scratch=()):
    return pl.pallas_call(
        kernel,
        out_shape=outs,
        in_specs=ins or [VMEM] * len(args),
        out_specs=out_specs or jax.tree.map(lambda _: VMEM, outs),
        scratch_shapes=scratch,
        compiler_params=pltpu.CompilerParams(vmem_limit_bytes=48 * 1024 * 1024),
        cost_estimate=pl.CostEstimate(
            flops=flops, bytes_accessed=nbytes, transcendentals=trans
        ),
    )(*args)


def pack_kernel(w_ref, wo_ref, out_ref, buf, sems):
    core = lax.axis_index("core")

    def put(first, second):
        loads = [
            pltpu.make_async_copy(first, buf.at[0], sems.at[4, 0]),
            pltpu.make_async_copy(second, buf.at[1], sems.at[4, 1]),
        ]
        for copy in loads:
            copy.start()
        copies = []
        for j in range(2):
            loads[j].wait()
            for i in range(4):
                copies.append(pltpu.make_async_copy(buf.at[j], out_ref.at[i, j], sems.at[i, j]))
                copies[-1].start()
        for copy in copies:
            copy.wait()

    @pl.when(core == 0)
    def _():
        put(w_ref.at[0], w_ref.at[1])

    @pl.when(core == 1)
    def _():
        put(w_ref.at[2], wo_ref)


def modulate(x_ref, shift, scale):
    x = x_ref[...].astype(F32)
    mean = jnp.sum(x, axis=-1, keepdims=True) * (1.0 / D)
    centered = x - mean
    var = jnp.sum(centered * centered, axis=-1, keepdims=True) * (1.0 / D)
    normed = centered * lax.rsqrt(var + 1e-06)
    return normed * (1.0 + scale) + shift


def norm_kernel(x_ref, xo_ref, shift_ref, scale_ref, out_ref):
    shift = shift_ref[...]
    scale = scale_ref[...]
    out_ref[:, :TOK] = modulate(x_ref, shift, scale).T.astype(BF)
    out_ref[:, TOK:] = modulate(xo_ref, shift, scale).T.astype(BF)


def qkv_kernel(mod_ref, mine_ref, other_ref, mine4_ref, other4_ref, out_ref, wo_ref, buf, sems, wsems):
    core = lax.axis_index("core")

    def go(qk_ref, vo_ref, vo4_ref):
        moves = [
            pltpu.make_async_copy(vo4_ref.at[h, 1], wo_ref.at[h], wsems.at[h]) for h in range(4)
        ]
        for move in moves:
            move.start()
        mod = mod_ref[...]
        qk = jnp.dot(qk_ref[...], mod, preferred_element_type=F32)
        vo = jnp.dot(vo_ref[...], mod, preferred_element_type=F32)
        for h in range(4):
            rows = jnp.concatenate(
                [qk[2 * HD * h : 2 * HD * (h + 1)], vo[2 * HD * h : 2 * HD * h + HD]], axis=0
            )
            buf[h] = rows.astype(BF)
            copy = pltpu.make_async_copy(buf.at[h], out_ref.at[h], sems.at[h])
            copy.start()
            moves.append(copy)
        for move in moves:
            move.wait()

    @pl.when(core == 0)
    def _():
        go(mine_ref, other_ref, other4_ref)

    @pl.when(core == 1)
    def _():
        go(other_ref, mine_ref, mine4_ref)


def attention_kernel(qkv_ref, out_ref, buf, sems):
    yhi = lax.axis_index("yhi")
    factor = math.log2(math.e) * HD**-0.5
    keys = []
    values = []
    queries = []
    ones = jnp.ones((8, 2 * TOK), F32)
    for b in range(4):
        block = qkv_ref[b].astype(F32)
        q = block[:HD] * factor
        hi = q.astype(BF).astype(F32)
        lo = q - hi
        k = block[HD : 2 * HD]
        both = jnp.concatenate([hi, lo], axis=0).astype(BF)
        queries.append((both[:, :TOK], b, 0))
        queries.append((both[:, TOK:], b, 1))
        kt = k.T.astype(BF)
        keys.append(jnp.concatenate([kt, kt], axis=1))
        values.append(jnp.concatenate([block[2 * HD :], ones], axis=0).astype(BF))

    def score(i):
        return [jnp.dot(k, queries[i][0], preferred_element_type=F32) for k in keys]

    copies = []
    ahead = score(0)
    for i in range(8):
        s = ahead
        if i < 7:
            ahead = score(i + 1)
        peak = functools.reduce(jnp.maximum, [jnp.max(c, axis=0, keepdims=True) for c in s])
        o = sum(
            jnp.dot(v, jnp.exp2(c - peak).astype(BF), preferred_element_type=F32)
            for c, v in zip(s, values)
        )
        _, b, half = queries[i]
        slot = (yhi if half == 0 else 1 - yhi) * 4 + b
        buf[i] = (o[:HD] / o[HD : HD + 1]).astype(BF)
        copies.append(pltpu.make_async_copy(buf.at[i], out_ref.at[slot], sems.at[i]))
        copies[-1].start()
    for copy in copies:
        copy.wait()


def column(row):
    size = row.shape[1]
    eye = lax.broadcasted_iota(jnp.int32, (size, size), 0) == lax.broadcasted_iota(
        jnp.int32, (size, size), 1
    )
    return jnp.sum(jnp.where(eye, row.astype(F32), 0.0), axis=1, keepdims=True)


def ordered(east_ref, west_ref):
    first = lax.axis_index("core") == 0
    east = east_ref[...]
    west = west_ref[...]
    return jnp.where(first, east, west), jnp.where(first, west, east)


def select_rows(east_ref, west_ref):
    a, b = ordered(east_ref, west_ref)
    rows = jnp.concatenate([column(a), column(b)], axis=0).astype(jnp.int32)
    return jnp.where(
        lax.broadcasted_iota(jnp.int32, (2 * OV, TOK), 1) == rows, 1.0, 0.0
    ).astype(BF)


def project(attn, wo):
    return lax.dot_general(attn, wo, (((0,), (0,)), ((), ())), preferred_element_type=F32)


def margin_kernel(attn_ref, wo_ref, wo2_ref, x_ref, gate_ref, east_ref, west_ref, a_ref, b_ref):
    yhi = lax.axis_index("yhi")
    pick = select_rows(east_ref, west_ref)
    nt = (((1,), (1,)), ((), ()))
    mine = lax.dot_general(pick, attn_ref[yhi], nt, preferred_element_type=F32).astype(BF)
    other = lax.dot_general(pick, attn_ref[1 - yhi], nt, preferred_element_type=F32).astype(BF)
    x = jnp.dot(pick, x_ref[...], preferred_element_type=F32)
    proj = jnp.dot(mine, wo_ref[...], preferred_element_type=F32) + jnp.dot(
        other, wo2_ref[...], preferred_element_type=F32
    )
    rows = (x + gate_ref[...] * proj).astype(BF)
    a_ref[...] = rows[:OV]
    b_ref[...] = rows[OV:]


def out_kernel(attn_ref, wo_ref, wo2_ref, x_ref, gate_ref, out_ref):
    yhi = lax.axis_index("yhi")
    proj = project(attn_ref[yhi], wo_ref[...]) + project(attn_ref[1 - yhi], wo2_ref[...])
    out_ref[...] = (x_ref[...].astype(F32) + gate_ref[...] * proj).astype(BF)


def blend_kernel(lay_ref, a_ref, b_ref, ra_ref, rb_ref, east_ref, west_ref, bw_ref, out_ref):
    core = lax.axis_index("core")
    tile = lax.axis_index("z") * 4 + lax.axis_index("ylo") * 2 + core
    prior = jnp.where(tile == 0, 63, tile - 1)
    east = column(bw_ref[pl.ds(tile, 1), :])
    west = 8.0 - column(bw_ref[pl.ds(prior, 1), :])
    own_a = jnp.where(core == 0, east, west)
    own_b = jnp.where(core == 0, west, east)
    new_a = (own_a * a_ref[...].astype(F32) + (8.0 - own_a) * ra_ref[...].astype(F32)) / 8.0
    new_b = (own_b * b_ref[...].astype(F32) + (8.0 - own_b) * rb_ref[...].astype(F32)) / 8.0
    new = jnp.concatenate([new_a, new_b], axis=0).astype(BF)
    index = jnp.concatenate(ordered(east_ref, west_ref), axis=1)
    hot = jnp.where(
        lax.broadcasted_iota(jnp.int32, (TOK, 2 * OV), 0) == index, 1.0, 0.0
    )
    mask = jnp.sum(hot, axis=1, keepdims=True)
    placed = jnp.dot(hot.astype(BF), new, preferred_element_type=F32)
    out_ref[...] = jnp.where(mask > 0.5, placed, lay_ref[...].astype(F32)).astype(BF)


def body(tokens, mod_shift, mod_scale, mod_gate, w_qkv, w_out, east_rows, west_rows, blend_weight):
    sds = jax.ShapeDtypeStruct
    dma = pltpu.SemaphoreType.DMA
    x = tokens[0]
    swap = [(0, 1), (1, 0)]
    x_other = lax.ppermute(x, "yhi", swap)
    packed = call(
        pack_kernel,
        pltpu.HBM((4, 2, HD, D), BF),
        tuple(
            pltpu.with_memory_space_constraint(w, pltpu.HBM)
            for w in (jnp.transpose(w_qkv, (0, 2, 1)), w_out)
        ),
        1000,
        2000000,
        ins=[HBM, HBM],
        out_specs=HBM,
        scratch=[pltpu.VMEM((2, HD, D), BF), dma((5, 2))],
    )
    mine = lax.all_to_all(packed, "x", 0, 0, tiled=True)
    mine, x_other = lax.optimization_barrier((mine, x_other))
    other = lax.ppermute(mine, "core", swap)
    mod = call(
        norm_kernel,
        sds((D, 2 * TOK), BF),
        (x, x_other, mod_shift, mod_scale),
        20 * 512 * D,
        3000000,
    )
    qkv, wo = call(
        qkv_kernel,
        (pltpu.HBM((4, 3 * HD, 2 * TOK), BF), sds((4, HD, D), BF)),
        (mod, mine.reshape(8 * HD, D), other.reshape(8 * HD, D), mine, other),
        2 * 512 * 1152 * D,
        6000000,
        out_specs=(HBM, VMEM),
        scratch=[pltpu.VMEM((4, 3 * HD, 2 * TOK), BF), dma((4,)), dma((4,))],
    )
    pairs = [(0, 3), (3, 0), (1, 2), (2, 1)]
    wo_other = lax.ppermute(wo, ("ylo", "yhi"), pairs)
    qkv = lax.all_to_all(qkv, "x", 0, 0, tiled=True)
    attn = call(
        attention_kernel,
        pltpu.HBM((8, HD, TOK), BF),
        (qkv,),
        4 * 2048 * 2048 * 128,
        1500000,
        2048 * 2048,
        out_specs=HBM,
        scratch=[pltpu.VMEM((8, HD, TOK), BF), dma((8,))],
    )
    attn = lax.all_to_all(attn, ("yhi", "x"), 0, 0, tiled=True).reshape(2, 4 * HD, TOK)
    wo = wo.reshape(4 * HD, D)
    wo_other = wo_other.reshape(4 * HD, D)
    a, b = call(
        margin_kernel,
        (sds((OV, D), BF), sds((OV, D), BF)),
        (attn, wo, wo_other, x, mod_gate, east_rows, west_rows),
        2 * 64 * 576 * D,
        2000000,
    )
    other_b = lax.ppermute(b, TILE, [(i, (i + 2 * (i % 2) - 1) % 64) for i in range(64)])
    other_a = lax.ppermute(a, TILE, [(i, i + 1 - 2 * (i % 2)) for i in range(64)])
    lay = call(
        out_kernel,
        sds((TOK, D), BF),
        (attn, wo, wo_other, x, mod_gate),
        2 * 256 * 576 * D,
        3000000,
    )
    out = call(
        blend_kernel,
        sds((TOK, D), BF),
        (lay, a, b, other_a, other_b, east_rows, west_rows, blend_weight),
        2 * 256 * 64 * D,
        1500000,
    )
    return out[None]


def solution(mesh):
    fine = Mesh(mesh.devices.reshape(16, 2, 2, 4, 2), ("z", "ylo", "core", "x", "yhi"))
    in_specs = (
        P(TILE, SEQ, None),
        P(TILE, None),
        P(TILE, None),
        P(TILE, None),
        P(None, None, SEQ),
        P(SEQ, None),
        P(TILE, SEQ),
        P(TILE, SEQ),
        P(None, SEQ),
    )
    out_specs = P(TILE, SEQ, None)
    return jax.shard_map(body, mesh=fine, in_specs=in_specs, out_specs=out_specs, check_vma=False)
```

```python
import functools
import math

import jax
import jax.numpy as jnp
from jax import lax
from jax.experimental import pallas as pl
from jax.experimental.pallas import tpu as pltpu
from jax.sharding import Mesh
from jax.sharding import PartitionSpec as P

D = 1152
HD = 72
TOK = 256
OV = 32
TILE = ("z", "ylo", "core")
SEQ = ("x", "yhi")
VMEM = pl.BlockSpec(memory_space=pltpu.VMEM)
HBM = pl.BlockSpec(memory_space=pltpu.HBM)
BF = jnp.bfloat16
F32 = jnp.float32


def call(kernel, outs, args, flops, nbytes, trans=0, ins=None, out_specs=None, scratch=()):
    return pl.pallas_call(
        kernel,
        out_shape=outs,
        in_specs=ins or [VMEM] * len(args),
        out_specs=out_specs or jax.tree.map(lambda _: VMEM, outs),
        scratch_shapes=scratch,
        compiler_params=pltpu.CompilerParams(vmem_limit_bytes=48 * 1024 * 1024),
        cost_estimate=pl.CostEstimate(
            flops=flops, bytes_accessed=nbytes, transcendentals=trans
        ),
    )(*args)


def pack_kernel(w_ref, wo_ref, out_ref, buf, sems):
    core = lax.axis_index("core")

    def put(first, second):
        loads = [
            pltpu.make_async_copy(first, buf.at[0], sems.at[4, 0]),
            pltpu.make_async_copy(second, buf.at[1], sems.at[4, 1]),
        ]
        for copy in loads:
            copy.start()
        copies = []
        for j in range(2):
            loads[j].wait()
            for i in range(4):
                copies.append(pltpu.make_async_copy(buf.at[j], out_ref.at[i, j], sems.at[i, j]))
                copies[-1].start()
        for copy in copies:
            copy.wait()

    @pl.when(core == 0)
    def _():
        put(w_ref.at[0], w_ref.at[1])

    @pl.when(core == 1)
    def _():
        put(w_ref.at[2], wo_ref)


def modulate(x_ref, shift, scale):
    x = x_ref[...].astype(F32)
    mean = jnp.sum(x, axis=-1, keepdims=True) * (1.0 / D)
    centered = x - mean
    var = jnp.sum(centered * centered, axis=-1, keepdims=True) * (1.0 / D)
    normed = centered * lax.rsqrt(var + 1e-06)
    return (normed * (1.0 + scale) + shift).astype(BF)


def column(row):
    size = row.shape[1]
    eye = lax.broadcasted_iota(jnp.int32, (size, size), 0) == lax.broadcasted_iota(
        jnp.int32, (size, size), 1
    )
    return jnp.sum(jnp.where(eye, row.astype(F32), 0.0), axis=1, keepdims=True)


def margin_rows(east, west):
    rows = jnp.concatenate([column(east), column(west)], axis=0).astype(jnp.int32)
    token = lax.broadcasted_iota(jnp.int32, (2 * OV, TOK), 1)
    return jnp.where(token == rows, 1.0, 0.0)


def token_order(east, west):
    margin = margin_rows(east, west)
    rest = 1.0 - jnp.sum(margin, axis=0, keepdims=True)
    before = lax.broadcasted_iota(jnp.int32, (TOK, TOK), 0) < lax.broadcasted_iota(
        jnp.int32, (TOK, TOK), 1
    )
    rank = jnp.dot(
        jnp.broadcast_to(rest, (16, TOK)).astype(BF),
        jnp.where(before, 1.0, 0.0).astype(BF),
        preferred_element_type=F32,
    )[:1].astype(jnp.int32)
    place = lax.broadcasted_iota(jnp.int32, (TOK - 2 * OV, TOK), 0)
    others = jnp.where(place == rank, rest, 0.0)
    return jnp.concatenate([margin, others], axis=0).astype(BF)


def norm_kernel(x_ref, xo_ref, shift_ref, scale_ref, east_ref, west_ref, oidx_ref, out_ref, perm_ref):
    shift = shift_ref[...]
    scale = scale_ref[...]
    mine = token_order(east_ref[...], west_ref[...])
    other = token_order(oidx_ref[:, :OV], oidx_ref[:, OV:])
    perm_ref[...] = mine
    a = jnp.dot(mine, modulate(x_ref, shift, scale), preferred_element_type=F32)
    b = jnp.dot(other, modulate(xo_ref, shift, scale), preferred_element_type=F32)
    m = 2 * OV
    out_ref[:, : 2 * m] = jnp.concatenate([a[:m], b[:m]], axis=0).T.astype(BF)
    out_ref[:, 2 * m :] = jnp.concatenate([a[m:], b[m:]], axis=0).T.astype(BF)


def qkv_kernel(mod_ref, mine_ref, other_ref, mine4_ref, other4_ref, out_ref, wo_ref, buf, sems, wsems):
    core = lax.axis_index("core")

    def go(qk_ref, vo_ref, vo4_ref):
        moves = [
            pltpu.make_async_copy(vo4_ref.at[h, 1], wo_ref.at[h], wsems.at[h]) for h in range(4)
        ]
        for move in moves:
            move.start()
        mod = mod_ref[...]
        qk = jnp.dot(qk_ref[...], mod, preferred_element_type=F32)
        vo = jnp.dot(vo_ref[...], mod, preferred_element_type=F32)
        for h in range(4):
            rows = jnp.concatenate(
                [qk[2 * HD * h : 2 * HD * (h + 1)], vo[2 * HD * h : 2 * HD * h + HD]], axis=0
            )
            buf[h] = rows.astype(BF)
            copy = pltpu.make_async_copy(buf.at[h], out_ref.at[h], sems.at[h])
            copy.start()
            moves.append(copy)
        for move in moves:
            move.wait()

    @pl.when(core == 0)
    def _():
        go(mine_ref, other_ref, other4_ref)

    @pl.when(core == 1)
    def _():
        go(other_ref, mine_ref, mine4_ref)


def attend(queries, keys, values, count, finish):
    def score(i):
        return [jnp.dot(k, queries(i), preferred_element_type=F32) for k in keys]

    ahead = score(0)
    for i in range(count):
        s = ahead
        if i + 1 < count:
            ahead = score(i + 1)
        peak = functools.reduce(jnp.maximum, [jnp.max(c, axis=0, keepdims=True) for c in s])
        o = sum(
            jnp.dot(v, jnp.exp2(c - peak).astype(BF), preferred_element_type=F32)
            for c, v in zip(s, values)
        )
        finish(i, (o[:HD] / o[HD : HD + 1]).astype(BF))


def margin_attention_kernel(qkv_ref, out_ref, k_ref, v_ref, q_ref, buf, sems):
    factor = math.log2(math.e) * HD**-0.5
    keys = []
    values = []
    first = []
    ones = jnp.ones((8, 2 * TOK), F32)
    for b in range(4):
        block = qkv_ref[b].astype(F32)
        q = block[:HD] * factor
        hi = q.astype(BF).astype(F32)
        lo = q - hi
        both = jnp.concatenate([hi, lo], axis=0).astype(BF)
        first.append(both[:, :128])
        q_ref[:, 384 * b : 384 * (b + 1)] = both[:, 128:]
        kt = block[HD : 2 * HD].T.astype(BF)
        keys.append(jnp.concatenate([kt, kt], axis=1))
        k_ref[b] = keys[b]
        values.append(jnp.concatenate([block[2 * HD :], ones], axis=0).astype(BF))
        v_ref[b] = values[b]
    groups = [jnp.concatenate(first[:2], axis=1), jnp.concatenate(first[2:], axis=1)]
    copies = []

    def finish(i, o):
        for j in range(2):
            b = 2 * i + j
            buf[b] = o[:, 128 * j : 128 * (j + 1)]
            for half in range(2):
                copies.append(
                    pltpu.make_async_copy(buf.at[b], out_ref.at[4 * half + b], sems.at[4 * half + b])
                )
                copies[-1].start()

    attend(lambda i: groups[i], keys, values, 2, finish)
    for copy in copies:
        copy.wait()


def attention_kernel(k_ref, v_ref, q_ref, out_ref, buf, sems):
    yhi = lax.axis_index("yhi")
    keys = [k_ref[b] for b in range(4)]
    values = [v_ref[b] for b in range(4)]
    ready = {1: (0,), 2: (1,), 4: (2,), 5: (3,)}
    copies = []

    def finish(i, o):
        buf[:, TOK * i : TOK * (i + 1)] = o
        for b in ready.get(i, ()):
            for half in range(2):
                slot = (yhi if half == 0 else 1 - yhi) * 4 + b
                copies.append(
                    pltpu.make_async_copy(
                        buf.at[:, pl.ds(384 * b + 128 * half, TOK)],
                        out_ref.at[slot],
                        sems.at[4 * half + b],
                    )
                )
                copies[-1].start()

    attend(lambda i: q_ref[:, TOK * i : TOK * (i + 1)], keys, values, 6, finish)
    for copy in copies:
        copy.wait()


def project(attn, wo):
    return lax.dot_general(attn, wo, (((0,), (0,)), ((), ())), preferred_element_type=F32)


def margin_kernel(attn_ref, wo_ref, wo2_ref, x_ref, gate_ref, east_ref, west_ref, a_ref, b_ref):
    yhi = lax.axis_index("yhi")
    first = lax.axis_index("core") == 0
    pick = margin_rows(east_ref[...], west_ref[...]).astype(BF)
    x = jnp.dot(pick, x_ref[...], preferred_element_type=F32)
    m = 2 * OV
    proj = project(attn_ref[yhi], wo_ref[...])[:m] + project(attn_ref[1 - yhi], wo2_ref[...])[m:]
    rows = x + gate_ref[...] * proj
    a_ref[...] = jnp.where(first, rows[:OV], rows[OV:]).astype(BF)
    b_ref[...] = jnp.where(first, rows[OV:], rows[:OV]).astype(BF)


def out_kernel(attn_ref, wo_ref, wo2_ref, x_ref, gate_ref, perm_ref, out_ref):
    yhi = lax.axis_index("yhi")
    m = 2 * OV
    proj = (
        project(attn_ref[yhi], wo_ref[...])[: TOK - m]
        + project(attn_ref[1 - yhi], wo2_ref[...])[m:]
    )
    x = jnp.dot(perm_ref[m:], x_ref[...], preferred_element_type=F32)
    out_ref[...] = (x + gate_ref[...] * proj).astype(BF)


def blend_kernel(rest_ref, a_ref, b_ref, ra_ref, rb_ref, perm_ref, bw_ref, out_ref):
    core = lax.axis_index("core")
    tile = lax.axis_index("z") * 4 + lax.axis_index("ylo") * 2 + core
    prior = jnp.where(tile == 0, 63, tile - 1)
    east = column(bw_ref[pl.ds(tile, 1), :])
    west = 8.0 - column(bw_ref[pl.ds(prior, 1), :])
    own_a = jnp.where(core == 0, east, west)
    own_b = jnp.where(core == 0, west, east)
    new_a = (own_a * a_ref[...].astype(F32) + (8.0 - own_a) * ra_ref[...].astype(F32)) / 8.0
    new_b = (own_b * b_ref[...].astype(F32) + (8.0 - own_b) * rb_ref[...].astype(F32)) / 8.0
    new_e = jnp.where(core == 0, new_a, new_b)
    new_w = jnp.where(core == 0, new_b, new_a)
    rows = jnp.concatenate([jnp.concatenate([new_e, new_w], axis=0).astype(BF), rest_ref[...]], axis=0)
    out_ref[...] = project(perm_ref[...], rows).astype(BF)


def body(tokens, mod_shift, mod_scale, mod_gate, w_qkv, w_out, east_rows, west_rows, blend_weight):
    sds = jax.ShapeDtypeStruct
    dma = pltpu.SemaphoreType.DMA
    x = tokens[0]
    swap = [(0, 1), (1, 0)]
    x_other = lax.ppermute(x, "yhi", swap)
    packed = call(
        pack_kernel,
        pltpu.HBM((4, 2, HD, D), BF),
        tuple(
            pltpu.with_memory_space_constraint(w, pltpu.HBM)
            for w in (jnp.transpose(w_qkv, (0, 2, 1)), w_out)
        ),
        1000,
        2000000,
        ins=[HBM, HBM],
        out_specs=HBM,
        scratch=[pltpu.VMEM((2, HD, D), BF), dma((5, 2))],
    )
    mine = lax.all_to_all(packed, "x", 0, 0, tiled=True)
    other_rows = lax.ppermute(jnp.concatenate([east_rows, west_rows], axis=1), "yhi", swap)
    mine, x_other, other_rows = lax.optimization_barrier((mine, x_other, other_rows))
    other = lax.ppermute(mine, "core", swap)
    mod, perm = call(
        norm_kernel,
        (sds((D, 2 * TOK), BF), sds((TOK, TOK), BF)),
        (x, x_other, mod_shift, mod_scale, east_rows, west_rows, other_rows),
        2 * 512 * 256 * D,
        3000000,
    )
    qkv, wo = call(
        qkv_kernel,
        (pltpu.HBM((4, 3 * HD, 2 * TOK), BF), sds((4, HD, D), BF)),
        (mod, mine.reshape(8 * HD, D), other.reshape(8 * HD, D), mine, other),
        2 * 512 * 1152 * D,
        6000000,
        out_specs=(HBM, VMEM),
        scratch=[pltpu.VMEM((4, 3 * HD, 2 * TOK), BF), dma((4,)), dma((4,))],
    )
    pairs = [(0, 3), (3, 0), (1, 2), (2, 1)]
    wo_other = lax.ppermute(wo, ("ylo", "yhi"), pairs)
    qkv = lax.all_to_all(qkv, "x", 0, 0, tiled=True)
    margins, keys, values, queries = call(
        margin_attention_kernel,
        (
            pltpu.HBM((8, HD, 128), BF),
            sds((4, 2 * TOK, 2 * HD), BF),
            sds((4, HD + 8, 2 * TOK), BF),
            sds((2 * HD, 1536), BF),
        ),
        (qkv,),
        4 * 512 * 2048 * 128,
        3000000,
        512 * 2048,
        out_specs=(HBM, VMEM, VMEM, VMEM),
        scratch=[pltpu.VMEM((4, HD, 128), BF), dma((8,))],
    )
    margins = lax.all_to_all(margins, ("yhi", "x"), 0, 0, tiled=True)
    attn = call(
        attention_kernel,
        pltpu.HBM((8, HD, TOK), BF),
        (keys, values, queries),
        4 * 1536 * 2048 * 128,
        2500000,
        1536 * 2048,
        out_specs=HBM,
        scratch=[pltpu.VMEM((HD, 1536), BF), dma((8,))],
    )
    margins, _ = lax.optimization_barrier((margins, attn))
    margins = margins.reshape(2, 4 * HD, 128)
    attn = lax.all_to_all(attn, ("yhi", "x"), 0, 0, tiled=True).reshape(2, 4 * HD, TOK)
    wo = wo.reshape(4 * HD, D)
    wo_other = wo_other.reshape(4 * HD, D)
    a, b = call(
        margin_kernel,
        (sds((OV, D), BF), sds((OV, D), BF)),
        (margins, wo, wo_other, x, mod_gate, east_rows, west_rows),
        2 * 128 * 576 * D,
        2000000,
    )
    other_b = lax.ppermute(b, TILE, [(i, (i + 2 * (i % 2) - 1) % 64) for i in range(64)])
    other_a = lax.ppermute(a, TILE, [(i, i + 1 - 2 * (i % 2)) for i in range(64)])
    rest = call(
        out_kernel,
        sds((TOK - 2 * OV, D), BF),
        (attn, wo, wo_other, x, mod_gate, perm),
        2 * 256 * 832 * D,
        3000000,
    )
    out = call(
        blend_kernel,
        sds((TOK, D), BF),
        (rest, a, b, other_a, other_b, perm, blend_weight),
        2 * 256 * 256 * D,
        1500000,
    )
    return out[None]


def solution(mesh):
    fine = Mesh(mesh.devices.reshape(16, 2, 2, 4, 2), ("z", "ylo", "core", "x", "yhi"))
    in_specs = (
        P(TILE, SEQ, None),
        P(TILE, None),
        P(TILE, None),
        P(TILE, None),
        P(None, None, SEQ),
        P(SEQ, None),
        P(TILE, SEQ),
        P(TILE, SEQ),
        P(None, SEQ),
    )
    out_specs = P(TILE, SEQ, None)
    return jax.shard_map(body, mesh=fine, in_specs=in_specs, out_specs=out_specs, check_vma=False)
```

```python
import functools
import math

import jax
import jax.numpy as jnp
from jax import lax
from jax.experimental import pallas as pl
from jax.experimental.pallas import tpu as pltpu
from jax.sharding import Mesh
from jax.sharding import PartitionSpec as P

D = 1152
HD = 72
TOK = 256
OV = 32
TILE = ("z", "ylo", "core")
SEQ = ("x", "yhi")
VMEM = pl.BlockSpec(memory_space=pltpu.VMEM)
HBM = pl.BlockSpec(memory_space=pltpu.HBM)
BF = jnp.bfloat16
F32 = jnp.float32


def call(kernel, outs, args, flops, nbytes, trans=0, ins=None, out_specs=None, scratch=()):
    return pl.pallas_call(
        kernel,
        out_shape=outs,
        in_specs=ins or [VMEM] * len(args),
        out_specs=out_specs or jax.tree.map(lambda _: VMEM, outs),
        scratch_shapes=scratch,
        compiler_params=pltpu.CompilerParams(vmem_limit_bytes=48 * 1024 * 1024),
        cost_estimate=pl.CostEstimate(
            flops=flops, bytes_accessed=nbytes, transcendentals=trans
        ),
    )(*args)


def pack_kernel(w_ref, wo_ref, out_ref, sems):
    core = lax.axis_index("core")

    def put(first, second):
        copies = [
            pltpu.make_async_copy(first, out_ref.at[0], sems.at[0]),
            pltpu.make_async_copy(second, out_ref.at[1], sems.at[1]),
        ]
        for copy in copies:
            copy.start()
        for copy in copies:
            copy.wait()

    @pl.when(core == 0)
    def _():
        put(w_ref.at[0], w_ref.at[1])

    @pl.when(core == 1)
    def _():
        put(w_ref.at[2], wo_ref)


def modulate(x_ref, shift, scale):
    x = x_ref[...].astype(F32)
    mean = jnp.sum(x, axis=-1, keepdims=True) * (1.0 / D)
    centered = x - mean
    var = jnp.sum(centered * centered, axis=-1, keepdims=True) * (1.0 / D)
    normed = centered * lax.rsqrt(var + 1e-06)
    return normed * (1.0 + scale) + shift


def norm_kernel(x_ref, xo_ref, shift_ref, scale_ref, out_ref):
    shift = shift_ref[...]
    scale = scale_ref[...]
    out_ref[:, :TOK] = modulate(x_ref, shift, scale).T.astype(BF)
    out_ref[:, TOK:] = modulate(xo_ref, shift, scale).T.astype(BF)


def half_kernel(mod_ref, w0_ref, w1_ref, w2_ref, w3_ref, out_ref):
    mod = mod_ref[...]
    for d, w_ref in enumerate((w0_ref, w1_ref, w2_ref, w3_ref)):
        out_ref[d] = jnp.dot(w_ref[...], mod, preferred_element_type=F32).astype(BF)


def qkv_kernel(mod_ref, half_ref, *refs):
    others, mine3, other3 = refs[:4], refs[4:8], refs[8:12]
    outs, wo_ref, sems = refs[12:16], refs[16], refs[17]
    core = lax.axis_index("core")
    x = lax.axis_index("x")

    def moved(pieces):
        moves = [
            pltpu.make_async_copy(
                pieces[d].at[1], wo_ref.at[lax.rem(x + d, 4)], sems.at[d]
            )
            for d in range(4)
        ]
        for move in moves:
            move.start()
        return moves

    @pl.when(core == 0)
    def _():
        moves = moved(other3)
        mod = mod_ref[...]
        for d in range(4):
            v = jnp.dot(others[d][:80], mod, preferred_element_type=F32)[:HD]
            outs[d][...] = jnp.concatenate([half_ref[d].astype(F32), v], axis=0).astype(BF)
        for move in moves:
            move.wait()

    @pl.when(core == 1)
    def _():
        moves = moved(mine3)
        mod = mod_ref[...]
        for d in range(4):
            qk = jnp.dot(others[d][...], mod, preferred_element_type=F32)
            v = half_ref[d].astype(F32)[:HD]
            outs[d][...] = jnp.concatenate([qk, v], axis=0).astype(BF)
        for move in moves:
            move.wait()


def attention_kernel(q0_ref, q1_ref, q2_ref, q3_ref, out_ref, buf, sems):
    yhi = lax.axis_index("yhi")
    x = lax.axis_index("x")
    factor = math.log2(math.e) * HD**-0.5
    keys = []
    values = []
    queries = []
    ones = jnp.ones((8, 2 * TOK), F32)
    for b in range(4):
        block = (q0_ref, q1_ref, q2_ref, q3_ref)[b][...].astype(F32)
        q = block[:HD] * factor
        hi = q.astype(BF).astype(F32)
        lo = q - hi
        k = block[HD : 2 * HD]
        both = jnp.concatenate([hi, lo], axis=0).astype(BF)
        queries.append((both[:, :TOK], b, 0))
        queries.append((both[:, TOK:], b, 1))
        kt = k.T.astype(BF)
        keys.append(jnp.concatenate([kt, kt], axis=1))
        values.append(jnp.concatenate([block[2 * HD :], ones], axis=0).astype(BF))

    def score(i):
        return [jnp.dot(k, queries[i][0], preferred_element_type=F32) for k in keys]

    copies = []
    ahead = score(0)
    for i in range(8):
        s = ahead
        if i < 7:
            ahead = score(i + 1)
        peak = functools.reduce(jnp.maximum, [jnp.max(c, axis=0, keepdims=True) for c in s])
        o = sum(
            jnp.dot(v, jnp.exp2(c - peak).astype(BF), preferred_element_type=F32)
            for c, v in zip(s, values)
        )
        _, b, half = queries[i]
        slot = (yhi if half == 0 else 1 - yhi) * 4 + lax.rem(x + 4 - b, 4)
        buf[i] = (o[:HD] / o[HD : HD + 1]).astype(BF)
        copies.append(pltpu.make_async_copy(buf.at[i], out_ref.at[slot], sems.at[i]))
        copies[-1].start()
    for copy in copies:
        copy.wait()


def column(row):
    size = row.shape[1]
    eye = lax.broadcasted_iota(jnp.int32, (size, size), 0) == lax.broadcasted_iota(
        jnp.int32, (size, size), 1
    )
    return jnp.sum(jnp.where(eye, row.astype(F32), 0.0), axis=1, keepdims=True)


def ordered(east_ref, west_ref):
    first = lax.axis_index("core") == 0
    east = east_ref[...]
    west = west_ref[...]
    return jnp.where(first, east, west), jnp.where(first, west, east)


def select_rows(east_ref, west_ref):
    a, b = ordered(east_ref, west_ref)
    rows = jnp.concatenate([column(a), column(b)], axis=0).astype(jnp.int32)
    return jnp.where(
        lax.broadcasted_iota(jnp.int32, (2 * OV, TOK), 1) == rows, 1.0, 0.0
    ).astype(BF)


def project(attn, wo):
    return lax.dot_general(attn, wo, (((0,), (0,)), ((), ())), preferred_element_type=F32)


def margin_kernel(attn_ref, wo_ref, wo2_ref, x_ref, gate_ref, east_ref, west_ref, b_ref, a_ref):
    yhi = lax.axis_index("yhi")
    pick = select_rows(east_ref, west_ref)
    nt = (((1,), (1,)), ((), ()))
    mine = lax.dot_general(pick, attn_ref[yhi], nt, preferred_element_type=F32).astype(BF)
    other = lax.dot_general(pick, attn_ref[1 - yhi], nt, preferred_element_type=F32).astype(BF)
    x = jnp.dot(pick, x_ref[...], preferred_element_type=F32)
    proj = jnp.dot(mine, wo_ref[...], preferred_element_type=F32) + jnp.dot(
        other, wo2_ref[...], preferred_element_type=F32
    )
    rows = (x + gate_ref[...] * proj).astype(BF)
    a_ref[...] = rows[:OV]
    b_ref[...] = rows[OV:]


def out_kernel(attn_ref, wo_ref, wo2_ref, x_ref, gate_ref, out_ref):
    yhi = lax.axis_index("yhi")
    proj = project(attn_ref[yhi], wo_ref[...]) + project(attn_ref[1 - yhi], wo2_ref[...])
    out_ref[...] = (x_ref[...].astype(F32) + gate_ref[...] * proj).astype(BF)


def blend_kernel(lay_ref, b_ref, a_ref, rb_ref, ra_ref, east_ref, west_ref, bw_ref, out_ref):
    core = lax.axis_index("core")
    tile = lax.axis_index("z") * 4 + lax.axis_index("ylo") * 2 + core
    prior = jnp.where(tile == 0, 63, tile - 1)
    east = column(bw_ref[pl.ds(tile, 1), :])
    west = 8.0 - column(bw_ref[pl.ds(prior, 1), :])
    own_a = jnp.where(core == 0, east, west)
    own_b = jnp.where(core == 0, west, east)
    new_a = (own_a * a_ref[...].astype(F32) + (8.0 - own_a) * ra_ref[...].astype(F32)) / 8.0
    new_b = (own_b * b_ref[...].astype(F32) + (8.0 - own_b) * rb_ref[...].astype(F32)) / 8.0
    new = jnp.concatenate([new_a, new_b], axis=0).astype(BF)
    index = jnp.concatenate(ordered(east_ref, west_ref), axis=1)
    hot = jnp.where(
        lax.broadcasted_iota(jnp.int32, (TOK, 2 * OV), 0) == index, 1.0, 0.0
    )
    mask = jnp.sum(hot, axis=1, keepdims=True)
    placed = jnp.dot(hot.astype(BF), new, preferred_element_type=F32)
    out_ref[...] = jnp.where(mask > 0.5, placed, lay_ref[...].astype(F32)).astype(BF)


def body(tokens, mod_shift, mod_scale, mod_gate, w_qkv, w_out, east_rows, west_rows, blend_weight):
    sds = jax.ShapeDtypeStruct
    dma = pltpu.SemaphoreType.DMA
    x = tokens[0]
    swap = [(0, 1), (1, 0)]
    x_other = lax.ppermute(x, "yhi", swap)
    piece = call(
        pack_kernel,
        sds((2, HD, D), BF),
        tuple(
            pltpu.with_memory_space_constraint(w, pltpu.HBM)
            for w in (jnp.transpose(w_qkv, (0, 2, 1)), w_out)
        ),
        1000,
        600000,
        ins=[HBM, HBM],
        scratch=[dma((2,))],
    )

    def send(value, by):
        return lax.ppermute(value, "x", [(i, (i + by) % 4) for i in range(4)])

    mine = [piece, send(piece, -1), send(piece, -2), send(piece, -3)]
    other = [lax.ppermute(mine[d], "core", swap) for d in (0, 1, 3)]
    last, x_other, other = lax.optimization_barrier((mine[2], x_other, other))
    mine[2] = last
    other.insert(2, lax.ppermute(last, "core", swap))
    mod = call(
        norm_kernel,
        sds((D, 2 * TOK), BF),
        (x, x_other, mod_shift, mod_scale),
        20 * 512 * D,
        3000000,
    )
    half = call(
        half_kernel,
        sds((4, 2 * HD, 2 * TOK), BF),
        (mod, *[w.reshape(2 * HD, D) for w in mine]),
        2 * 512 * 576 * D,
        3000000,
    )
    *qkv, wo = call(
        qkv_kernel,
        (sds((3 * HD, 2 * TOK), BF),) * 4 + (sds((4, HD, D), BF),),
        (mod, half, *[w.reshape(2 * HD, D) for w in other], *mine, *other),
        2 * 512 * 576 * D,
        6000000,
        scratch=[dma((4,))],
    )
    pairs = [(0, 3), (3, 0), (1, 2), (2, 1)]
    wo_other = lax.ppermute(wo, ("ylo", "yhi"), pairs)
    qkv = [qkv[0]] + [send(qkv[d], d) for d in (1, 2, 3)]
    attn = call(
        attention_kernel,
        pltpu.HBM((8, HD, TOK), BF),
        tuple(qkv),
        4 * 2048 * 2048 * 128,
        1500000,
        2048 * 2048,
        out_specs=HBM,
        scratch=[pltpu.VMEM((8, HD, TOK), BF), dma((8,))],
    )
    attn = lax.all_to_all(attn, ("yhi", "x"), 0, 0, tiled=True).reshape(2, 4 * HD, TOK)
    wo = wo.reshape(4 * HD, D)
    wo_other = wo_other.reshape(4 * HD, D)
    b, a = call(
        margin_kernel,
        (sds((OV, D), BF), sds((OV, D), BF)),
        (attn, wo, wo_other, x, mod_gate, east_rows, west_rows),
        2 * 64 * 576 * D,
        2000000,
    )
    other_b = lax.ppermute(b, TILE, [(i, (i + 2 * (i % 2) - 1) % 64) for i in range(64)])
    other_a = lax.ppermute(a, TILE, [(i, i + 1 - 2 * (i % 2)) for i in range(64)])
    lay = call(
        out_kernel,
        sds((TOK, D), BF),
        (attn, wo, wo_other, x, mod_gate),
        2 * 256 * 576 * D,
        3000000,
    )
    out = call(
        blend_kernel,
        sds((TOK, D), BF),
        (lay, b, a, other_b, other_a, east_rows, west_rows, blend_weight),
        2 * 256 * 64 * D,
        1500000,
    )
    return out[None]


def solution(mesh):
    fine = Mesh(mesh.devices.reshape(16, 2, 2, 4, 2), ("z", "ylo", "core", "x", "yhi"))
    in_specs = (
        P(TILE, SEQ, None),
        P(TILE, None),
        P(TILE, None),
        P(TILE, None),
        P(None, None, SEQ),
        P(SEQ, None),
        P(TILE, SEQ),
        P(TILE, SEQ),
        P(None, SEQ),
    )
    out_specs = P(TILE, SEQ, None)
    return jax.shard_map(body, mesh=fine, in_specs=in_specs, out_specs=out_specs, check_vma=False)
```

```python
import functools
import math

import jax
import jax.numpy as jnp
from jax import lax
from jax.experimental import pallas as pl
from jax.experimental.pallas import tpu as pltpu
from jax.sharding import Mesh
from jax.sharding import PartitionSpec as P

D = 1152
HD = 72
TOK = 256
OV = 32
TILE = ("z", "ylo", "core")
SEQ = ("x", "yhi")
VMEM = pl.BlockSpec(memory_space=pltpu.VMEM)
HBM = pl.BlockSpec(memory_space=pltpu.HBM)
BF = jnp.bfloat16
F32 = jnp.float32


def call(kernel, outs, args, flops, nbytes, trans=0, ins=None, out_specs=None, scratch=()):
    return pl.pallas_call(
        kernel,
        out_shape=outs,
        in_specs=ins or [VMEM] * len(args),
        out_specs=out_specs or jax.tree.map(lambda _: VMEM, outs),
        scratch_shapes=scratch,
        compiler_params=pltpu.CompilerParams(vmem_limit_bytes=48 * 1024 * 1024),
        cost_estimate=pl.CostEstimate(
            flops=flops, bytes_accessed=nbytes, transcendentals=trans
        ),
    )(*args)


def pack_kernel(w_ref, wo_ref, out_ref, buf, sems):
    core = lax.axis_index("core")

    def put(first, second):
        loads = [
            pltpu.make_async_copy(first, buf.at[0], sems.at[4, 0]),
            pltpu.make_async_copy(second, buf.at[1], sems.at[4, 1]),
        ]
        for copy in loads:
            copy.start()
        copies = []
        for j in range(2):
            loads[j].wait()
            for i in range(4):
                copies.append(pltpu.make_async_copy(buf.at[j], out_ref.at[i, j], sems.at[i, j]))
                copies[-1].start()
        for copy in copies:
            copy.wait()

    @pl.when(core == 0)
    def _():
        put(w_ref.at[0], w_ref.at[1])

    @pl.when(core == 1)
    def _():
        put(w_ref.at[2], wo_ref)


def modulate(x_ref, shift, scale):
    x = x_ref[...].astype(F32)
    mean = jnp.sum(x, axis=-1, keepdims=True) * (1.0 / D)
    centered = x - mean
    var = jnp.sum(centered * centered, axis=-1, keepdims=True) * (1.0 / D)
    normed = centered * lax.rsqrt(var + 1e-06)
    return normed * (1.0 + scale) + shift


def norm_kernel(x_ref, xo_ref, shift_ref, scale_ref, out_ref):
    shift = shift_ref[...]
    scale = scale_ref[...]
    out_ref[:, :TOK] = modulate(x_ref, shift, scale).T.astype(BF)
    out_ref[:, TOK:] = modulate(xo_ref, shift, scale).T.astype(BF)


def half_kernel(mod_ref, w_ref, out_ref):
    out_ref[...] = jnp.dot(w_ref[...], mod_ref[...], preferred_element_type=F32).astype(BF)


def qkv_kernel(mod_ref, half_ref, other_ref, mine4_ref, other4_ref, out_ref, wo_ref, buf, sems, wsems):
    core = lax.axis_index("core")

    def go(vo4_ref, own_first):
        moves = [
            pltpu.make_async_copy(vo4_ref.at[h, 1], wo_ref.at[h], wsems.at[h]) for h in range(4)
        ]
        for move in moves:
            move.start()
        other = jnp.dot(other_ref[...], mod_ref[...], preferred_element_type=F32)
        for h in range(4):
            own = half_ref[2 * HD * h : 2 * HD * (h + 1)].astype(F32)
            swapped = other[2 * HD * h : 2 * HD * (h + 1)]
            qk, vo = (own, swapped) if own_first else (swapped, own)
            buf[h] = jnp.concatenate([qk, vo[:HD]], axis=0).astype(BF)
            copy = pltpu.make_async_copy(buf.at[h], out_ref.at[h], sems.at[h])
            copy.start()
            moves.append(copy)
        for move in moves:
            move.wait()

    @pl.when(core == 0)
    def _():
        go(other4_ref, True)

    @pl.when(core == 1)
    def _():
        go(mine4_ref, False)


def attention_kernel(qkv_ref, out_ref, buf, sems):
    yhi = lax.axis_index("yhi")
    factor = math.log2(math.e) * HD**-0.5
    keys = []
    values = []
    queries = []
    ones = jnp.ones((8, 2 * TOK), F32)
    for b in range(4):
        block = qkv_ref[b].astype(F32)
        q = block[:HD] * factor
        hi = q.astype(BF).astype(F32)
        lo = q - hi
        k = block[HD : 2 * HD]
        both = jnp.concatenate([hi, lo], axis=0).astype(BF)
        queries.append((both[:, :TOK], b, 0))
        queries.append((both[:, TOK:], b, 1))
        kt = k.T.astype(BF)
        keys.append(jnp.concatenate([kt, kt], axis=1))
        values.append(jnp.concatenate([block[2 * HD :], ones], axis=0).astype(BF))

    def score(i):
        return [jnp.dot(k, queries[i][0], preferred_element_type=F32) for k in keys]

    copies = []
    ahead = score(0)
    for i in range(8):
        s = ahead
        if i < 7:
            ahead = score(i + 1)
        peak = functools.reduce(jnp.maximum, [jnp.max(c, axis=0, keepdims=True) for c in s])
        o = sum(
            jnp.dot(v, jnp.exp2(c - peak).astype(BF), preferred_element_type=F32)
            for c, v in zip(s, values)
        )
        _, b, half = queries[i]
        slot = (yhi if half == 0 else 1 - yhi) * 4 + b
        buf[i] = (o[:HD] / o[HD : HD + 1]).astype(BF)
        copies.append(pltpu.make_async_copy(buf.at[i], out_ref.at[slot], sems.at[i]))
        copies[-1].start()
    for copy in copies:
        copy.wait()


def column(row):
    size = row.shape[1]
    eye = lax.broadcasted_iota(jnp.int32, (size, size), 0) == lax.broadcasted_iota(
        jnp.int32, (size, size), 1
    )
    return jnp.sum(jnp.where(eye, row.astype(F32), 0.0), axis=1, keepdims=True)


def select_rows(east_ref, west_ref):
    e = column(east_ref[...])
    w = column(west_ref[...])
    rows = jnp.concatenate([e, w], axis=0).astype(jnp.int32)
    return jnp.where(
        lax.broadcasted_iota(jnp.int32, (2 * OV, TOK), 1) == rows, 1.0, 0.0
    ).astype(BF)


def project(attn, wo):
    return lax.dot_general(attn, wo, (((0,), (0,)), ((), ())), preferred_element_type=F32)


def margin_kernel(attn_ref, wo_ref, wo2_ref, x_ref, gate_ref, east_ref, west_ref, w_ref, e_ref):
    yhi = lax.axis_index("yhi")
    pick = select_rows(east_ref, west_ref)
    nt = (((1,), (1,)), ((), ()))
    mine = lax.dot_general(pick, attn_ref[yhi], nt, preferred_element_type=F32).astype(BF)
    other = lax.dot_general(pick, attn_ref[1 - yhi], nt, preferred_element_type=F32).astype(BF)
    x = jnp.dot(pick, x_ref[...], preferred_element_type=F32)
    proj = jnp.dot(mine, wo_ref[...], preferred_element_type=F32) + jnp.dot(
        other, wo2_ref[...], preferred_element_type=F32
    )
    rows = (x + gate_ref[...] * proj).astype(BF)
    w_ref[...] = rows[OV:]
    e_ref[...] = rows[:OV]


def out_kernel(attn_ref, wo_ref, wo2_ref, x_ref, gate_ref, out_ref):
    yhi = lax.axis_index("yhi")
    proj = project(attn_ref[yhi], wo_ref[...]) + project(attn_ref[1 - yhi], wo2_ref[...])
    out_ref[...] = (x_ref[...].astype(F32) + gate_ref[...] * proj).astype(BF)


def blend_kernel(lay_ref, w_ref, e_ref, next_ref, prev_ref, east_ref, west_ref, bw_ref, out_ref):
    tile = lax.axis_index("z") * 4 + lax.axis_index("ylo") * 2 + lax.axis_index("core")
    prior = jnp.where(tile == 0, 63, tile - 1)
    a_e = column(bw_ref[pl.ds(tile, 1), :])
    a_w = column(bw_ref[pl.ds(prior, 1), :])
    new_e = (a_e * e_ref[...].astype(F32) + (8.0 - a_e) * next_ref[...].astype(F32)) / 8.0
    new_w = ((8.0 - a_w) * w_ref[...].astype(F32) + a_w * prev_ref[...].astype(F32)) / 8.0
    new = jnp.concatenate([new_e, new_w], axis=0).astype(BF)
    index = jnp.concatenate([east_ref[...], west_ref[...]], axis=1)
    hot = jnp.where(
        lax.broadcasted_iota(jnp.int32, (TOK, 2 * OV), 0) == index, 1.0, 0.0
    )
    mask = jnp.sum(hot, axis=1, keepdims=True)
    placed = jnp.dot(hot.astype(BF), new, preferred_element_type=F32)
    out_ref[...] = jnp.where(mask > 0.5, placed, lay_ref[...].astype(F32)).astype(BF)


def body(tokens, mod_shift, mod_scale, mod_gate, w_qkv, w_out, east_rows, west_rows, blend_weight):
    sds = jax.ShapeDtypeStruct
    dma = pltpu.SemaphoreType.DMA
    x = tokens[0]
    swap = [(0, 1), (1, 0)]
    x_other = lax.ppermute(x, "yhi", swap)
    packed = call(
        pack_kernel,
        pltpu.HBM((4, 2, HD, D), BF),
        tuple(
            pltpu.with_memory_space_constraint(w, pltpu.HBM)
            for w in (jnp.transpose(w_qkv, (0, 2, 1)), w_out)
        ),
        1000,
        2000000,
        ins=[HBM, HBM],
        out_specs=HBM,
        scratch=[pltpu.VMEM((2, HD, D), BF), dma((5, 2))],
    )
    mine = lax.all_to_all(packed, "x", 0, 0, tiled=True)
    mine, x_other = lax.optimization_barrier((mine, x_other))
    other = lax.ppermute(mine, "core", swap)
    mod = call(
        norm_kernel,
        sds((D, 2 * TOK), BF),
        (x, x_other, mod_shift, mod_scale),
        20 * 512 * D,
        3000000,
    )
    half = call(
        half_kernel,
        sds((8 * HD, 2 * TOK), BF),
        (mod, mine.reshape(8 * HD, D)),
        2 * 512 * 576 * D,
        2500000,
    )
    qkv, wo = call(
        qkv_kernel,
        (pltpu.HBM((4, 3 * HD, 2 * TOK), BF), sds((4, HD, D), BF)),
        (mod, half, other.reshape(8 * HD, D), mine, other),
        2 * 512 * 576 * D,
        5000000,
        out_specs=(HBM, VMEM),
        scratch=[pltpu.VMEM((4, 3 * HD, 2 * TOK), BF), dma((4,)), dma((4,))],
    )
    pairs = [(0, 3), (3, 0), (1, 2), (2, 1)]
    wo_other = lax.ppermute(wo, ("ylo", "yhi"), pairs)
    qkv = lax.all_to_all(qkv, "x", 0, 0, tiled=True)
    attn = call(
        attention_kernel,
        pltpu.HBM((8, HD, TOK), BF),
        (qkv,),
        4 * 2048 * 2048 * 128,
        1500000,
        2048 * 2048,
        out_specs=HBM,
        scratch=[pltpu.VMEM((8, HD, TOK), BF), dma((8,))],
    )
    attn = lax.all_to_all(attn, ("yhi", "x"), 0, 0, tiled=True).reshape(2, 4 * HD, TOK)
    wo = wo.reshape(4 * HD, D)
    wo_other = wo_other.reshape(4 * HD, D)
    own_w, own_e = call(
        margin_kernel,
        (sds((OV, D), BF), sds((OV, D), BF)),
        (attn, wo, wo_other, x, mod_gate, east_rows, west_rows),
        2 * 64 * 576 * D,
        2000000,
    )
    next_w = lax.ppermute(own_w, TILE, [(i, (i - 1) % 64) for i in range(64)])
    prev_e = lax.ppermute(own_e, TILE, [(i, (i + 1) % 64) for i in range(64)])
    lay = call(
        out_kernel,
        sds((TOK, D), BF),
        (attn, wo, wo_other, x, mod_gate),
        2 * 256 * 576 * D,
        3000000,
    )
    out = call(
        blend_kernel,
        sds((TOK, D), BF),
        (lay, own_w, own_e, next_w, prev_e, east_rows, west_rows, blend_weight),
        2 * 256 * 64 * D,
        1500000,
    )
    return out[None]


def solution(mesh):
    fine = Mesh(mesh.devices.reshape(16, 2, 2, 4, 2), ("z", "ylo", "core", "x", "yhi"))
    in_specs = (
        P(TILE, SEQ, None),
        P(TILE, None),
        P(TILE, None),
        P(TILE, None),
        P(None, None, SEQ),
        P(SEQ, None),
        P(TILE, SEQ),
        P(TILE, SEQ),
        P(None, SEQ),
    )
    out_specs = P(TILE, SEQ, None)
    return jax.shard_map(body, mesh=fine, in_specs=in_specs, out_specs=out_specs, check_vma=False)
```

```python
import functools
import math

import jax
import jax.numpy as jnp
from jax import lax
from jax.experimental import pallas as pl
from jax.experimental.pallas import tpu as pltpu
from jax.sharding import Mesh
from jax.sharding import PartitionSpec as P

D = 1152
HD = 72
TOK = 256
OV = 32
TILE = ("z", "ylo", "core")
SEQ = ("x", "yhi")
VMEM = pl.BlockSpec(memory_space=pltpu.VMEM)
HBM = pl.BlockSpec(memory_space=pltpu.HBM)
BF = jnp.bfloat16
F32 = jnp.float32


def call(kernel, outs, args, flops, nbytes, trans=0, ins=None, out_specs=None, scratch=()):
    return pl.pallas_call(
        kernel,
        out_shape=outs,
        in_specs=ins or [VMEM] * len(args),
        out_specs=out_specs or jax.tree.map(lambda _: VMEM, outs),
        scratch_shapes=scratch,
        compiler_params=pltpu.CompilerParams(vmem_limit_bytes=48 * 1024 * 1024),
        cost_estimate=pl.CostEstimate(
            flops=flops, bytes_accessed=nbytes, transcendentals=trans
        ),
    )(*args)


def pack_kernel(w_ref, wo_ref, out_ref, buf, sems):
    core = lax.axis_index("core")

    def put(first, second):
        loads = [
            pltpu.make_async_copy(first, buf.at[0], sems.at[4, 0]),
            pltpu.make_async_copy(second, buf.at[1], sems.at[4, 1]),
        ]
        for copy in loads:
            copy.start()
        copies = []
        for j in range(2):
            loads[j].wait()
            for i in range(4):
                copies.append(pltpu.make_async_copy(buf.at[j], out_ref.at[i, j], sems.at[i, j]))
                copies[-1].start()
        for copy in copies:
            copy.wait()

    @pl.when(core == 0)
    def _():
        put(w_ref.at[0], w_ref.at[1])

    @pl.when(core == 1)
    def _():
        put(w_ref.at[2], wo_ref)


def modulate(x_ref, shift, scale):
    x = x_ref[...].astype(F32)
    mean = jnp.sum(x, axis=-1, keepdims=True) * (1.0 / D)
    centered = x - mean
    var = jnp.sum(centered * centered, axis=-1, keepdims=True) * (1.0 / D)
    normed = centered * lax.rsqrt(var + 1e-06)
    return normed * (1.0 + scale) + shift


def norm_kernel(x_ref, xo_ref, shift_ref, scale_ref, out_ref):
    shift = shift_ref[...]
    scale = scale_ref[...]
    out_ref[:, :TOK] = modulate(x_ref, shift, scale).T.astype(BF)
    out_ref[:, TOK:] = modulate(xo_ref, shift, scale).T.astype(BF)


def half_kernel(mod_ref, w_ref, out_ref):
    out_ref[...] = jnp.dot(w_ref[...], mod_ref[...], preferred_element_type=F32).astype(BF)


def qkv_kernel(mod_ref, half_ref, other_ref, mine4_ref, other4_ref, out_ref, wo_ref, buf, sems, wsems):
    core = lax.axis_index("core")

    def go(vo4_ref, own_first):
        moves = [
            pltpu.make_async_copy(vo4_ref.at[h, 1], wo_ref.at[h], wsems.at[h]) for h in range(4)
        ]
        for move in moves:
            move.start()
        mod = mod_ref[...]
        for h in range(4):
            if h % 2 == 0:
                rows = other_ref[2 * HD * h : 2 * HD * (h + 2)]
                other = jnp.dot(rows, mod, preferred_element_type=F32)
            own = half_ref[2 * HD * h : 2 * HD * (h + 1)].astype(F32)
            swapped = other[2 * HD * (h % 2) : 2 * HD * (h % 2 + 1)]
            qk, vo = (own, swapped) if own_first else (swapped, own)
            buf[h] = jnp.concatenate([qk, vo[:HD]], axis=0).astype(BF)
            copy = pltpu.make_async_copy(buf.at[h], out_ref.at[h], sems.at[h])
            copy.start()
            moves.append(copy)
        for move in moves:
            move.wait()

    @pl.when(core == 0)
    def _():
        go(other4_ref, True)

    @pl.when(core == 1)
    def _():
        go(mine4_ref, False)


def attention_kernel(qkv_ref, out_ref, buf, sems):
    yhi = lax.axis_index("yhi")
    factor = math.log2(math.e) * HD**-0.5
    keys = []
    values = []
    queries = []
    ones = jnp.ones((8, 2 * TOK), F32)
    for b in range(4):
        block = qkv_ref[b].astype(F32)
        q = block[:HD] * factor
        hi = q.astype(BF).astype(F32)
        lo = q - hi
        k = block[HD : 2 * HD]
        both = jnp.concatenate([hi, lo], axis=0).astype(BF)
        queries.append((both[:, :TOK], b, 0))
        queries.append((both[:, TOK:], b, 1))
        kt = k.T.astype(BF)
        keys.append(jnp.concatenate([kt, kt], axis=1))
        values.append(jnp.concatenate([block[2 * HD :], ones], axis=0).astype(BF))

    def score(i):
        return [jnp.dot(k, queries[i][0], preferred_element_type=F32) for k in keys]

    copies = []
    ahead = score(0)
    for i in range(8):
        s = ahead
        if i < 7:
            ahead = score(i + 1)
        peak = functools.reduce(jnp.maximum, [jnp.max(c, axis=0, keepdims=True) for c in s])
        o = sum(
            jnp.dot(v, jnp.exp2(c - peak).astype(BF), preferred_element_type=F32)
            for c, v in zip(s, values)
        )
        _, b, half = queries[i]
        slot = (yhi if half == 0 else 1 - yhi) * 4 + b
        buf[i] = (o[:HD] / o[HD : HD + 1]).astype(BF)
        copies.append(pltpu.make_async_copy(buf.at[i], out_ref.at[slot], sems.at[i]))
        copies[-1].start()
    for copy in copies:
        copy.wait()


def column(row):
    size = row.shape[1]
    eye = lax.broadcasted_iota(jnp.int32, (size, size), 0) == lax.broadcasted_iota(
        jnp.int32, (size, size), 1
    )
    return jnp.sum(jnp.where(eye, row.astype(F32), 0.0), axis=1, keepdims=True)


def select_rows(east_ref, west_ref):
    e = column(east_ref[...])
    w = column(west_ref[...])
    rows = jnp.concatenate([e, w], axis=0).astype(jnp.int32)
    return jnp.where(
        lax.broadcasted_iota(jnp.int32, (2 * OV, TOK), 1) == rows, 1.0, 0.0
    ).astype(BF)


def project(attn, wo):
    return lax.dot_general(attn, wo, (((0,), (0,)), ((), ())), preferred_element_type=F32)


def margin_kernel(attn_ref, wo_ref, wo2_ref, x_ref, gate_ref, east_ref, west_ref, e_ref, w_ref):
    yhi = lax.axis_index("yhi")
    pick = select_rows(east_ref, west_ref)
    nt = (((1,), (1,)), ((), ()))
    mine = lax.dot_general(pick, attn_ref[yhi], nt, preferred_element_type=F32).astype(BF)
    other = lax.dot_general(pick, attn_ref[1 - yhi], nt, preferred_element_type=F32).astype(BF)
    x = jnp.dot(pick, x_ref[...], preferred_element_type=F32)
    proj = jnp.dot(mine, wo_ref[...], preferred_element_type=F32) + jnp.dot(
        other, wo2_ref[...], preferred_element_type=F32
    )
    rows = (x + gate_ref[...] * proj).astype(BF)
    w_ref[...] = rows[OV:]
    e_ref[...] = rows[:OV]


def out_kernel(attn_ref, wo_ref, wo2_ref, x_ref, gate_ref, out_ref):
    yhi = lax.axis_index("yhi")
    proj = project(attn_ref[yhi], wo_ref[...]) + project(attn_ref[1 - yhi], wo2_ref[...])
    out_ref[...] = (x_ref[...].astype(F32) + gate_ref[...] * proj).astype(BF)


def blend_kernel(lay_ref, e_ref, w_ref, prev_ref, next_ref, east_ref, west_ref, bw_ref, out_ref):
    tile = lax.axis_index("z") * 4 + lax.axis_index("ylo") * 2 + lax.axis_index("core")
    prior = jnp.where(tile == 0, 63, tile - 1)
    a_e = column(bw_ref[pl.ds(tile, 1), :])
    a_w = column(bw_ref[pl.ds(prior, 1), :])
    new_e = (a_e * e_ref[...].astype(F32) + (8.0 - a_e) * next_ref[...].astype(F32)) / 8.0
    new_w = ((8.0 - a_w) * w_ref[...].astype(F32) + a_w * prev_ref[...].astype(F32)) / 8.0
    new = jnp.concatenate([new_e, new_w], axis=0).astype(BF)
    index = jnp.concatenate([east_ref[...], west_ref[...]], axis=1)
    hot = jnp.where(
        lax.broadcasted_iota(jnp.int32, (TOK, 2 * OV), 0) == index, 1.0, 0.0
    )
    mask = jnp.sum(hot, axis=1, keepdims=True)
    placed = jnp.dot(hot.astype(BF), new, preferred_element_type=F32)
    out_ref[...] = jnp.where(mask > 0.5, placed, lay_ref[...].astype(F32)).astype(BF)


def body(tokens, mod_shift, mod_scale, mod_gate, w_qkv, w_out, east_rows, west_rows, blend_weight):
    sds = jax.ShapeDtypeStruct
    dma = pltpu.SemaphoreType.DMA
    x = tokens[0]
    swap = [(0, 1), (1, 0)]
    x_other = lax.ppermute(x, "yhi", swap)
    packed = call(
        pack_kernel,
        pltpu.HBM((4, 2, HD, D), BF),
        tuple(
            pltpu.with_memory_space_constraint(w, pltpu.HBM)
            for w in (jnp.transpose(w_qkv, (0, 2, 1)), w_out)
        ),
        1000,
        2000000,
        ins=[HBM, HBM],
        out_specs=HBM,
        scratch=[pltpu.VMEM((2, HD, D), BF), dma((5, 2))],
    )
    mine = lax.all_to_all(packed, "x", 0, 0, tiled=True)
    mine, x_other = lax.optimization_barrier((mine, x_other))
    other = lax.ppermute(mine, "core", swap)
    mod = call(
        norm_kernel,
        sds((D, 2 * TOK), BF),
        (x, x_other, mod_shift, mod_scale),
        20 * 512 * D,
        3000000,
    )
    half = call(
        half_kernel,
        sds((8 * HD, 2 * TOK), BF),
        (mod, mine.reshape(8 * HD, D)),
        2 * 512 * 576 * D,
        2500000,
    )
    qkv, wo = call(
        qkv_kernel,
        (pltpu.HBM((4, 3 * HD, 2 * TOK), BF), sds((4, HD, D), BF)),
        (mod, half, other.reshape(8 * HD, D), mine, other),
        2 * 512 * 576 * D,
        5000000,
        out_specs=(HBM, VMEM),
        scratch=[pltpu.VMEM((4, 3 * HD, 2 * TOK), BF), dma((4,)), dma((4,))],
    )
    pairs = [(0, 3), (3, 0), (1, 2), (2, 1)]
    wo_other = lax.ppermute(wo, ("ylo", "yhi"), pairs)
    qkv = lax.all_to_all(qkv, "x", 0, 0, tiled=True)
    attn = call(
        attention_kernel,
        pltpu.HBM((8, HD, TOK), BF),
        (qkv,),
        4 * 2048 * 2048 * 128,
        1500000,
        2048 * 2048,
        out_specs=HBM,
        scratch=[pltpu.VMEM((8, HD, TOK), BF), dma((8,))],
    )
    attn = lax.all_to_all(attn, ("yhi", "x"), 0, 0, tiled=True).reshape(2, 4 * HD, TOK)
    wo = wo.reshape(4 * HD, D)
    wo_other = wo_other.reshape(4 * HD, D)
    own_e, own_w = call(
        margin_kernel,
        (sds((OV, D), BF), sds((OV, D), BF)),
        (attn, wo, wo_other, x, mod_gate, east_rows, west_rows),
        2 * 64 * 576 * D,
        2000000,
    )
    prev_e = lax.ppermute(own_e, TILE, [(i, (i + 1) % 64) for i in range(64)])
    next_w = lax.ppermute(own_w, TILE, [(i, (i - 1) % 64) for i in range(64)])
    lay = call(
        out_kernel,
        sds((TOK, D), BF),
        (attn, wo, wo_other, x, mod_gate),
        2 * 256 * 576 * D,
        3000000,
    )
    out = call(
        blend_kernel,
        sds((TOK, D), BF),
        (lay, own_e, own_w, prev_e, next_w, east_rows, west_rows, blend_weight),
        2 * 256 * 64 * D,
        1500000,
    )
    return out[None]


def solution(mesh):
    fine = Mesh(mesh.devices.reshape(16, 2, 2, 4, 2), ("z", "ylo", "core", "x", "yhi"))
    in_specs = (
        P(TILE, SEQ, None),
        P(TILE, None),
        P(TILE, None),
        P(TILE, None),
        P(None, None, SEQ),
        P(SEQ, None),
        P(TILE, SEQ),
        P(TILE, SEQ),
        P(None, SEQ),
    )
    out_specs = P(TILE, SEQ, None)
    return jax.shard_map(body, mesh=fine, in_specs=in_specs, out_specs=out_specs, check_vma=False)
```

```python
import functools
import math

import jax
import jax.numpy as jnp
from jax import lax
from jax.experimental import pallas as pl
from jax.experimental.pallas import tpu as pltpu
from jax.sharding import Mesh
from jax.sharding import PartitionSpec as P

D = 1152
HD = 72
TOK = 256
OV = 32
TILE = ("z", "ylo", "core")
SEQ = ("x", "yhi")
VMEM = pl.BlockSpec(memory_space=pltpu.VMEM)
HBM = pl.BlockSpec(memory_space=pltpu.HBM)
BF = jnp.bfloat16
F32 = jnp.float32


def call(kernel, outs, args, flops, nbytes, trans=0, ins=None, out_specs=None, scratch=()):
    return pl.pallas_call(
        kernel,
        out_shape=outs,
        in_specs=ins or [VMEM] * len(args),
        out_specs=out_specs or jax.tree.map(lambda _: VMEM, outs),
        scratch_shapes=scratch,
        compiler_params=pltpu.CompilerParams(vmem_limit_bytes=48 * 1024 * 1024),
        cost_estimate=pl.CostEstimate(
            flops=flops, bytes_accessed=nbytes, transcendentals=trans
        ),
    )(*args)


def pack_kernel(w_ref, wo_ref, out_ref, buf, sems):
    core = lax.axis_index("core")

    def put(first, second):
        loads = [
            pltpu.make_async_copy(first, buf.at[0], sems.at[4, 0]),
            pltpu.make_async_copy(second, buf.at[1], sems.at[4, 1]),
        ]
        for copy in loads:
            copy.start()
        copies = []
        for j in range(2):
            loads[j].wait()
            for i in range(4):
                copies.append(pltpu.make_async_copy(buf.at[j], out_ref.at[i, j], sems.at[i, j]))
                copies[-1].start()
        for copy in copies:
            copy.wait()

    @pl.when(core == 0)
    def _():
        put(w_ref.at[0], w_ref.at[1])

    @pl.when(core == 1)
    def _():
        put(w_ref.at[2], wo_ref)


def modulate(x_ref, shift, scale):
    x = x_ref[...].astype(F32)
    mean = jnp.sum(x, axis=-1, keepdims=True) * (1.0 / D)
    centered = x - mean
    var = jnp.sum(centered * centered, axis=-1, keepdims=True) * (1.0 / D)
    normed = centered * lax.rsqrt(var + 1e-06)
    return normed * (1.0 + scale) + shift


def norm_kernel(x_ref, xo_ref, shift_ref, scale_ref, out_ref):
    shift = shift_ref[...]
    scale = scale_ref[...]
    out_ref[:, :TOK] = modulate(x_ref, shift, scale).T.astype(BF)
    out_ref[:, TOK:] = modulate(xo_ref, shift, scale).T.astype(BF)


def half_kernel(mod_ref, w_ref, out_ref):
    out_ref[...] = jnp.dot(w_ref[...], mod_ref[...], preferred_element_type=F32).astype(BF)


def qkv_kernel(mod_ref, half_ref, other_ref, mine4_ref, other4_ref, out_ref, wo_ref, buf, sems, wsems):
    core = lax.axis_index("core")

    def go(vo4_ref, own_first):
        moves = [
            pltpu.make_async_copy(vo4_ref.at[h, 1], wo_ref.at[h], wsems.at[h]) for h in range(4)
        ]
        for move in moves:
            move.start()
        mod = mod_ref[...]
        for h in range(4):
            if h % 2 == 0:
                rows = other_ref[2 * HD * h : 2 * HD * (h + 2)]
                other = jnp.dot(rows, mod, preferred_element_type=F32)
            own = half_ref[2 * HD * h : 2 * HD * (h + 1)].astype(F32)
            swapped = other[2 * HD * (h % 2) : 2 * HD * (h % 2 + 1)]
            qk, vo = (own, swapped) if own_first else (swapped, own)
            buf[h] = jnp.concatenate([qk, vo[:HD]], axis=0).astype(BF)
            copy = pltpu.make_async_copy(buf.at[h], out_ref.at[h], sems.at[h])
            copy.start()
            moves.append(copy)
        for move in moves:
            move.wait()

    @pl.when(core == 0)
    def _():
        go(other4_ref, True)

    @pl.when(core == 1)
    def _():
        go(mine4_ref, False)


def attention_kernel(qkv_ref, out_ref, buf, sems):
    yhi = lax.axis_index("yhi")
    factor = math.log2(math.e) * HD**-0.5
    keys = []
    values = []
    queries = []
    ones = jnp.ones((8, 2 * TOK), F32)
    for b in range(4):
        block = qkv_ref[b].astype(F32)
        q = block[:HD] * factor
        hi = q.astype(BF).astype(F32)
        lo = q - hi
        k = block[HD : 2 * HD]
        both = jnp.concatenate([hi, lo], axis=0).astype(BF)
        queries.append(both)
        kt = k.T.astype(BF)
        keys.append(jnp.concatenate([kt, kt], axis=1))
        values.append(jnp.concatenate([block[2 * HD :], ones], axis=0).astype(BF))

    def score(i):
        return [jnp.dot(k, queries[i], preferred_element_type=F32) for k in keys]

    copies = []
    ahead = score(0)
    for b in range(4):
        s = ahead
        if b < 3:
            ahead = score(b + 1)
        peak = functools.reduce(jnp.maximum, [jnp.max(c, axis=0, keepdims=True) for c in s])
        o = sum(
            jnp.dot(v, jnp.exp2(c - peak).astype(BF), preferred_element_type=F32)
            for c, v in zip(s, values)
        )
        res = (o[:HD] / o[HD : HD + 1]).astype(BF)
        for half in range(2):
            i = 2 * b + half
            slot = (yhi if half == 0 else 1 - yhi) * 4 + b
            buf[i] = res[:, half * TOK : (half + 1) * TOK]
            copies.append(pltpu.make_async_copy(buf.at[i], out_ref.at[slot], sems.at[i]))
            copies[-1].start()
    for copy in copies:
        copy.wait()


def column(row):
    size = row.shape[1]
    eye = lax.broadcasted_iota(jnp.int32, (size, size), 0) == lax.broadcasted_iota(
        jnp.int32, (size, size), 1
    )
    return jnp.sum(jnp.where(eye, row.astype(F32), 0.0), axis=1, keepdims=True)


def select_rows(east_ref, west_ref):
    e = column(east_ref[...])
    w = column(west_ref[...])
    rows = jnp.concatenate([e, w], axis=0).astype(jnp.int32)
    return jnp.where(
        lax.broadcasted_iota(jnp.int32, (2 * OV, TOK), 1) == rows, 1.0, 0.0
    ).astype(BF)


def project(attn, wo):
    return lax.dot_general(attn, wo, (((0,), (0,)), ((), ())), preferred_element_type=F32)


def margin_kernel(attn_ref, wo_ref, wo2_ref, x_ref, gate_ref, east_ref, west_ref, e_ref, w_ref):
    yhi = lax.axis_index("yhi")
    pick = select_rows(east_ref, west_ref)
    nt = (((1,), (1,)), ((), ()))
    mine = lax.dot_general(pick, attn_ref[yhi], nt, preferred_element_type=F32).astype(BF)
    other = lax.dot_general(pick, attn_ref[1 - yhi], nt, preferred_element_type=F32).astype(BF)
    x = jnp.dot(pick, x_ref[...], preferred_element_type=F32)
    proj = jnp.dot(mine, wo_ref[...], preferred_element_type=F32) + jnp.dot(
        other, wo2_ref[...], preferred_element_type=F32
    )
    rows = (x + gate_ref[...] * proj).astype(BF)
    w_ref[...] = rows[OV:]
    e_ref[...] = rows[:OV]


def out_kernel(attn_ref, wo_ref, wo2_ref, x_ref, gate_ref, out_ref):
    yhi = lax.axis_index("yhi")
    proj = project(attn_ref[yhi], wo_ref[...]) + project(attn_ref[1 - yhi], wo2_ref[...])
    out_ref[...] = (x_ref[...].astype(F32) + gate_ref[...] * proj).astype(BF)


def blend_kernel(lay_ref, e_ref, w_ref, prev_ref, next_ref, east_ref, west_ref, bw_ref, out_ref):
    tile = lax.axis_index("z") * 4 + lax.axis_index("ylo") * 2 + lax.axis_index("core")
    prior = jnp.where(tile == 0, 63, tile - 1)
    a_e = column(bw_ref[pl.ds(tile, 1), :])
    a_w = column(bw_ref[pl.ds(prior, 1), :])
    new_e = (a_e * e_ref[...].astype(F32) + (8.0 - a_e) * next_ref[...].astype(F32)) / 8.0
    new_w = ((8.0 - a_w) * w_ref[...].astype(F32) + a_w * prev_ref[...].astype(F32)) / 8.0
    new = jnp.concatenate([new_e, new_w], axis=0).astype(BF)
    index = jnp.concatenate([east_ref[...], west_ref[...]], axis=1)
    hot = jnp.where(
        lax.broadcasted_iota(jnp.int32, (TOK, 2 * OV), 0) == index, 1.0, 0.0
    )
    mask = jnp.sum(hot, axis=1, keepdims=True)
    placed = jnp.dot(hot.astype(BF), new, preferred_element_type=F32)
    out_ref[...] = jnp.where(mask > 0.5, placed, lay_ref[...].astype(F32)).astype(BF)


def body(tokens, mod_shift, mod_scale, mod_gate, w_qkv, w_out, east_rows, west_rows, blend_weight):
    sds = jax.ShapeDtypeStruct
    dma = pltpu.SemaphoreType.DMA
    x = tokens[0]
    swap = [(0, 1), (1, 0)]
    x_other = lax.ppermute(x, "yhi", swap)
    packed = call(
        pack_kernel,
        pltpu.HBM((4, 2, HD, D), BF),
        tuple(
            pltpu.with_memory_space_constraint(w, pltpu.HBM)
            for w in (jnp.transpose(w_qkv, (0, 2, 1)), w_out)
        ),
        1000,
        2000000,
        ins=[HBM, HBM],
        out_specs=HBM,
        scratch=[pltpu.VMEM((2, HD, D), BF), dma((5, 2))],
    )
    mine = lax.all_to_all(packed, "x", 0, 0, tiled=True)
    mine, x_other = lax.optimization_barrier((mine, x_other))
    other = lax.ppermute(mine, "core", swap)
    mod = call(
        norm_kernel,
        sds((D, 2 * TOK), BF),
        (x, x_other, mod_shift, mod_scale),
        20 * 512 * D,
        3000000,
    )
    half = call(
        half_kernel,
        sds((8 * HD, 2 * TOK), BF),
        (mod, mine.reshape(8 * HD, D)),
        2 * 512 * 576 * D,
        2500000,
    )
    qkv, wo = call(
        qkv_kernel,
        (pltpu.HBM((4, 3 * HD, 2 * TOK), BF), sds((4, HD, D), BF)),
        (mod, half, other.reshape(8 * HD, D), mine, other),
        2 * 512 * 576 * D,
        5000000,
        out_specs=(HBM, VMEM),
        scratch=[pltpu.VMEM((4, 3 * HD, 2 * TOK), BF), dma((4,)), dma((4,))],
    )
    pairs = [(0, 3), (3, 0), (1, 2), (2, 1)]
    wo_other = lax.ppermute(wo, ("ylo", "yhi"), pairs)
    qkv = lax.all_to_all(qkv, "x", 0, 0, tiled=True)
    attn = call(
        attention_kernel,
        pltpu.HBM((8, HD, TOK), BF),
        (qkv,),
        4 * 2048 * 2048 * 128,
        1500000,
        2048 * 2048,
        out_specs=HBM,
        scratch=[pltpu.VMEM((8, HD, TOK), BF), dma((8,))],
    )
    attn = lax.all_to_all(attn, ("yhi", "x"), 0, 0, tiled=True).reshape(2, 4 * HD, TOK)
    wo = wo.reshape(4 * HD, D)
    wo_other = wo_other.reshape(4 * HD, D)
    own_e, own_w = call(
        margin_kernel,
        (sds((OV, D), BF), sds((OV, D), BF)),
        (attn, wo, wo_other, x, mod_gate, east_rows, west_rows),
        2 * 64 * 576 * D,
        2000000,
    )
    prev_e = lax.ppermute(own_e, TILE, [(i, (i + 1) % 64) for i in range(64)])
    next_w = lax.ppermute(own_w, TILE, [(i, (i - 1) % 64) for i in range(64)])
    lay = call(
        out_kernel,
        sds((TOK, D), BF),
        (attn, wo, wo_other, x, mod_gate),
        2 * 256 * 576 * D,
        3000000,
    )
    out = call(
        blend_kernel,
        sds((TOK, D), BF),
        (lay, own_e, own_w, prev_e, next_w, east_rows, west_rows, blend_weight),
        2 * 256 * 64 * D,
        1500000,
    )
    return out[None]


def solution(mesh):
    fine = Mesh(mesh.devices.reshape(16, 2, 2, 4, 2), ("z", "ylo", "core", "x", "yhi"))
    in_specs = (
        P(TILE, SEQ, None),
        P(TILE, None),
        P(TILE, None),
        P(TILE, None),
        P(None, None, SEQ),
        P(SEQ, None),
        P(TILE, SEQ),
        P(TILE, SEQ),
        P(None, SEQ),
    )
    out_specs = P(TILE, SEQ, None)
    return jax.shard_map(body, mesh=fine, in_specs=in_specs, out_specs=out_specs, check_vma=False)
```
